256 devices in a mesh: tile: 64 (over x, z_lo, y), exp: 4 (over z_hi, core).
Axes of the slice: x: 4, y: 4, z: 8 (z_hi: 2, z_lo: 4; z = z_hi * 4 + z_lo), core: 2. Of those that a mesh axis runs over, the one named last changes fastest.
Arguments:
- template: bfloat16 [64, 256, 256], P('tile', 'exp'), may hold values from -8 to 8
- exposures: bfloat16 [64, 16, 256, 256], P('tile', 'exp'), may hold values from -20 to 20
- masks: int32 [64, 16, 256, 256], P('tile', 'exp'), may hold values 0 or 1
- basis_rows: float32 [27, 21], replicated, may hold values from -1.2 to 2.7
- basis_cols: float32 [27, 21], replicated, may hold values from -1.2 to 2.7
- psf_row: float32 [21], replicated, may hold values from 0 to 0.5
- psf_col: float32 [21], replicated, may hold values from 0 to 0.5
Outputs:
- coadd: float32 [64, 256, 256], P('tile', 'exp')
The draws below stay inside these ranges and needn't reach their ends.
All inputs are finite; a program needn't handle non-finite values. No bound on the sum of `masks` on one device may be relied on, other than what follows from the above.
Results may differ from the reference program's by a relative error of at most 0.0077.
Values may be sent and summed in bfloat16 or wider, within the bound.
No kernel may reach another device: no remote copies, remote signals or barrier semaphores. Data moves between devices by JAX's collectives and lax.ppermute only.
A program may use at most 128 MiB of HBM per device.

```python
import jax
import jax.numpy as jnp
from jax import lax

TPIX = 256
HW = 10
KW = 21
NB = 27
GW = 8
EXPOSURES = 16
TILES = 64


def shared_sky(key):
    base = jax.random.normal(key, (TILES, TPIX, TPIX), jnp.float32)
    return jnp.clip(base, -8.0, 8.0)


def draw_template(key, part):
    sky_tiles = shared_sky(key)
    return sky_tiles.astype(jnp.bfloat16)


def draw_exposures(key, part):
    sky_tiles = shared_sky(key)
    key = jax.random.fold_in(key, 2)
    gain_key, noise_key = jax.random.split(key)
    gains = jax.random.uniform(gain_key, (TILES, EXPOSURES, 1, 1), jnp.float32, 0.5, 2.0)
    noise = jax.random.normal(noise_key, (TILES, EXPOSURES, TPIX, TPIX), jnp.float32)
    return jnp.clip(gains * sky_tiles[:, None] + 0.5 * noise, -20.0, 20.0).astype(jnp.bfloat16)


def kernel_taps(key):
    tap_key, centre_key = jax.random.split(key)
    spread_taps = jnp.clip(0.3 * jax.random.normal(tap_key, (NB, KW), jnp.float32), -1.2, 1.2)
    centre = jax.random.uniform(centre_key, (NB, 1), jnp.float32, 0.5, 1.5)
    marker = (jnp.arange(KW) == HW).astype(jnp.float32)[None, :]
    return spread_taps * (1.0 - marker) + (spread_taps + centre) * marker


def draw_basis_rows(key, part):
    key = jax.random.fold_in(key, 3)
    return kernel_taps(key)


def draw_basis_cols(key, part):
    key = jax.random.fold_in(key, 4)
    return kernel_taps(key)


def plant(result, own_key, least, high):
    index_at = [jax.random.randint(jax.random.fold_in(own_key, axis), (), 0, length) for axis, length in enumerate(result.shape)]
    main_axis = result.shape.index(max(result.shape))
    beside = index_at[:main_axis] + [(index_at[main_axis] + 1) % result.shape[main_axis]] + index_at[main_axis + 1:]
    return result.at[tuple(index_at)].set(least).at[tuple(beside)].set(high)


def setup_inputs(seed: int = 0) -> dict:
    streams_of = jax.random.split(jax.random.key(seed), 8)
    template = draw_template(jax.random.fold_in(streams_of[7], 71), 0)
    exposures = draw_exposures(jax.random.fold_in(streams_of[7], 71), 0)
    masks = plant((jax.random.randint(streams_of[2], (TILES, EXPOSURES, TPIX, TPIX), 0, 4) < 1).astype(jnp.int32), jax.random.fold_in(streams_of[2], 1), 0, 1)
    basis_rows = draw_basis_rows(jax.random.fold_in(streams_of[7], 71), 0)
    basis_cols = draw_basis_cols(jax.random.fold_in(streams_of[7], 71), 0)
    psf_row = jnp.clip(jax.random.uniform(streams_of[5], (KW,), jnp.float32, 0.0, 0.5), 0.0, 0.5)
    psf_col = jnp.clip(jax.random.uniform(streams_of[6], (KW,), jnp.float32, 0.0, 0.5), 0.0, 0.5)
    return {"template": template, "exposures": exposures, "masks": masks, "basis_rows": basis_rows, "basis_cols": basis_cols, "psf_row": psf_row, "psf_col": psf_col}


def sky_of(tiles):
    grid_rows = TILES // GW
    return tiles.reshape(grid_rows, GW, TPIX, TPIX).transpose(0, 2, 1, 3).reshape(grid_rows * TPIX, GW * TPIX)

def tiles_of(image):
    grid_rows = TILES // GW
    return image.reshape(grid_rows, TPIX, GW, TPIX).transpose(0, 2, 1, 3).reshape(TILES, TPIX, TPIX)

def widen(values):
    return lax.optimization_barrier(values.astype(jnp.bfloat16)).astype(jnp.float32)

def reference(template, exposures, masks, basis_rows, basis_cols, psf_row, psf_col):
    sky_padded = jnp.pad(sky_of(template.astype(jnp.float32)), HW)
    row_taps = widen(basis_rows)
    col_taps = widen(basis_cols)

    def fit_tile(tile_index):
        grid_row = (tile_index // GW).astype(jnp.int32)
        grid_col = (tile_index % GW).astype(jnp.int32)
        window = lax.dynamic_slice(sky_padded, (grid_row * TPIX, grid_col * TPIX), (TPIX + 2 * HW, TPIX + 2 * HW))
        column_pass = jnp.zeros((NB, TPIX + 2 * HW, TPIX), jnp.float32)
        for shift_v in range(KW):
            column_pass = column_pass + col_taps[:, shift_v, None, None] * window[None, :, shift_v:shift_v + TPIX]
        column_pass = widen(column_pass)
        basis_img = jnp.zeros((NB, TPIX, TPIX), jnp.float32)
        for shift_u in range(KW):
            basis_img = basis_img + row_taps[:, shift_u, None, None] * column_pass[:, shift_u:shift_u + TPIX, :]
        flat = basis_img.astype(jnp.bfloat16).reshape(NB, TPIX * TPIX)
        images = lax.dynamic_index_in_dim(exposures, tile_index, 0, False)
        valid = lax.dynamic_index_in_dim(masks, tile_index, 0, False)

        def fit_exposure(inputs):
            exposure, mask_now = inputs
            exposure = exposure.reshape(-1)
            mask_flat = mask_now.reshape(-1)
            masked = flat * mask_flat.astype(jnp.bfloat16)[None, :]
            normal = jnp.dot(masked.astype(jnp.float32), flat.T.astype(jnp.float32), preferred_element_type=jnp.float32)
            right_side = jnp.dot(masked.astype(jnp.float32), exposure.astype(jnp.float32), preferred_element_type=jnp.float32)
            factor = jnp.linalg.cholesky(normal)
            coefficients = jax.scipy.linalg.cho_solve((factor, True), right_side).astype(jnp.bfloat16)
            model = jnp.dot(coefficients.astype(jnp.float32), flat.astype(jnp.float32), preferred_element_type=jnp.float32)
            difference = mask_flat.astype(jnp.float32) * (exposure.astype(jnp.float32) - model)
            return difference.astype(jnp.bfloat16).reshape(TPIX, TPIX)
        return lax.map(fit_exposure, (images, valid))
    differences = lax.map(fit_tile, jnp.arange(TILES, dtype=jnp.int32))
    height = TILES // GW * TPIX
    breadth = GW * TPIX

    def add_filtered(summed, slot_index):
        plane = lax.dynamic_index_in_dim(differences, slot_index, 1, False)
        padded = jnp.pad(sky_of(plane.astype(jnp.float32)), HW)
        column_pass = jnp.zeros((height + 2 * HW, breadth), jnp.float32)
        for shift_v in range(KW):
            column_pass = column_pass + psf_col[shift_v] * padded[:, shift_v:shift_v + breadth]
        filtered = jnp.zeros((height, breadth), jnp.float32)
        for shift_u in range(KW):
            filtered = filtered + psf_row[shift_u] * column_pass[shift_u:shift_u + height, :]
        return (summed + filtered, None)
    summed, unused = lax.scan(add_filtered, jnp.zeros((height, breadth), jnp.float32), jnp.arange(EXPOSURES, dtype=jnp.int32))
    coverage = sky_of(jnp.sum(masks.astype(jnp.float32), axis=1))
    return tiles_of(summed / jnp.maximum(coverage, 1.0))
```

```python
import jax
import jax.numpy as jnp
from jax import lax
from jax.experimental import pallas as pl
from jax.experimental.pallas import tpu as pltpu
from jax.sharding import PartitionSpec as P

HW = 10
KW = 21
NB = 27
GW = 8
PIX = 256
ROWS = 64
SLAB = 32
F32 = jnp.float32
BF16 = jnp.bfloat16


def toeplitz_rows(taps, rows):
    return pltpu.roll(jnp.broadcast_to(taps, (rows, taps.shape[1])), 0, 1, stride=1, stride_axis=0)


def fit_kernel(
    sky_ref, images_ref, masks_ref, row_taps_ref, col_taps_ref, out_ref,
    window, col_band, row_band, first, slab_wide, slab, plane,
):
    pieces = [sky_ref[k].astype(F32) for k in range(4)]
    window[...] = jnp.concatenate(
        [pieces[0][ROWS:ROWS + HW]] + [piece[:ROWS] for piece in pieces]
        + [pieces[3][ROWS:ROWS + HW], jnp.zeros((12, 384), F32)], 0
    ).astype(BF16)

    def build(b, carry):
        col = toeplitz_rows(col_taps_ref[pl.ds(b, 1), :], 256)
        col_band[b // 2, :, pl.ds(pl.multiple_of((b % 2) * 128, 128), 128)] = col[:, :128].astype(BF16)
        row_band[b] = toeplitz_rows(row_taps_ref[pl.ds(b, 1), :], 128).astype(BF16)
        return carry

    lax.fori_loop(0, NB + 1, build, 0)

    def columns(pair, carry):
        for half in range(2):
            out = jnp.dot(
                window[:, half * 128:half * 128 + 256], col_band[pair], preferred_element_type=F32
            ).astype(BF16)
            first[2 * pair, :, half * 128:half * 128 + 128] = out[:, :128]
            first[2 * pair + 1, :, half * 128:half * 128 + 128] = out[:, 128:]
        return carry

    lax.fori_loop(0, (NB + 1) // 2, columns, 0)

    for k in range(4):
        for half in range(2):
            slab_wide[half, pl.ds(NB + k, PIX, stride=SLAB), :] = images_ref[
                k, :, half * 128:half * 128 + 128
            ].astype(F32)
    for half in range(2):
        slab_wide[half, pl.ds(SLAB - 1, PIX, stride=SLAB), :] = jnp.zeros((PIX, 128), F32)

    def rows_pass(b, carry):
        for block in range(2):
            out = jnp.dot(
                row_band[b, :, :160], first[b, block * 128:block * 128 + 160, :],
                preferred_element_type=F32,
            )
            for half in range(2):
                slab_wide[half, pl.ds(block * 128 * SLAB + b, 128, stride=SLAB), :] = out[
                    :, half * 128:half * 128 + 128
                ]
        return carry

    lax.fori_loop(0, NB, rows_pass, 0)

    def gram(group, total):
        base = pl.multiple_of(group * 8 * SLAB, 8 * SLAB)
        at = pl.multiple_of(group * 8, 8)
        valid = [masks_ref[k, pl.ds(at, 8), :].astype(F32) for k in range(4)]
        for i in range(8):
            here = pl.ds(base + i * SLAB, SLAB)
            rows = jnp.concatenate([slab_wide[0, here, :], slab_wide[1, here, :]], 1)
            low = rows.astype(BF16)
            slab[here, :] = low
            masked = jnp.concatenate(
                [low * jnp.broadcast_to(v[i:i + 1].astype(BF16), low.shape) for v in valid], 0
            )
            total = total + lax.dot_general(
                low, masked, (((1,), (1,)), ((), ())), preferred_element_type=F32
            )
        return total

    matrix = lax.fori_loop(0, PIX // 8, gram, jnp.zeros((SLAB, 4 * SLAB), F32))

    lane = lax.broadcasted_iota(jnp.int32, (SLAB, 4 * SLAB), 1)
    row = lax.broadcasted_iota(jnp.int32, (SLAB, 4 * SLAB), 0)
    of_exposure = lane // SLAB
    of_basis = lane % SLAB
    for k in range(NB):
        column = jnp.take_along_axis(matrix, of_exposure * SLAB + k, axis=1)
        pivot_row = matrix[k:k + 1, :]
        pivot = column[k:k + 1, :]
        scaled = jnp.where(of_basis[:1] == k, 0.0, pivot_row / pivot)
        matrix = matrix - column * scaled
    top = jnp.sum(jnp.where(row == NB + of_exposure, matrix, 0.0), axis=0, keepdims=True)
    bottom = jnp.sum(jnp.where(row == of_basis, matrix, 0.0), axis=0, keepdims=True)
    solved = jnp.broadcast_to(top / bottom, (8, 4 * SLAB))
    lane8 = lax.broadcasted_iota(jnp.int32, (8, 4 * SLAB), 1)
    row8 = lax.broadcasted_iota(jnp.int32, (8, 4 * SLAB), 0)
    weights = []
    for k in range(4):
        own = -jnp.take_along_axis(solved, lane8 % SLAB + k * SLAB, axis=1)
        own = jnp.where(lane8 % SLAB == NB + k, 1.0, jnp.where(lane8 % SLAB >= NB, 0.0, own))
        weights.append(
            jnp.concatenate([jnp.where(row8 == lane8 // SLAB + 4 * half, own, 0.0) for half in range(2)], 1)
        )
    weights = jnp.concatenate(weights, 0).astype(BF16)

    plane[...] = jnp.zeros_like(plane)

    def residual(group, carry):
        base = pl.multiple_of(group * 8 * SLAB, 8 * SLAB)
        at = pl.multiple_of(group * 8, 8)
        left = jnp.dot(weights, slab[pl.ds(base, 8 * SLAB), :], preferred_element_type=F32)
        total = jnp.zeros((8, PIX), F32)
        for k in range(4):
            valid = masks_ref[k, pl.ds(at, 8), :].astype(F32)
            total = total + (valid * left[8 * k:8 * k + 8]).astype(BF16).astype(F32)
        plane[pl.ds(pl.multiple_of(group * 8 + 16, 8), 8), :] = total
        return carry

    lax.fori_loop(0, PIX // 8, residual, 0)
    for k in range(4):
        out_ref[k] = plane[64 * k + 6:64 * k + 6 + 96, :].astype(BF16)


def fit(sky, images, masks, row_taps, col_taps):
    vmem = pl.BlockSpec(memory_space=pltpu.VMEM)
    return pl.pallas_call(
        fit_kernel,
        out_shape=jax.ShapeDtypeStruct((4, 96, PIX), BF16),
        in_specs=[vmem] * 5,
        out_specs=vmem,
        scratch_shapes=[
            pltpu.VMEM((288, 384), BF16),
            pltpu.VMEM((14, 256, 256), BF16),
            pltpu.VMEM((28, 128, 256), BF16),
            pltpu.VMEM((28, 288, 256), BF16),
            pltpu.VMEM((2, PIX * SLAB, 128), F32),
            pltpu.VMEM((PIX * SLAB, 256), BF16),
            pltpu.VMEM((320, PIX), F32),
        ],
        compiler_params=pltpu.CompilerParams(vmem_limit_bytes=48 * 1024 * 1024),
        name="fit",
    )(sky, images, masks, row_taps, col_taps)


def filter_kernel(sky_ref, coverage_ref, row_taps_ref, col_taps_ref, out_ref):
    col_band = toeplitz_rows(col_taps_ref[...], 256)[:, :128]
    row_band = toeplitz_rows(row_taps_ref[...], ROWS)[:, :88]
    halves = [
        jnp.dot(sky_ref[:, half * 128:half * 128 + 256], col_band, precision=lax.Precision.HIGHEST,
                preferred_element_type=F32)
        for half in range(2)
    ]
    column_pass = jnp.concatenate(halves, 1)
    summed = jnp.dot(row_band, column_pass, precision=lax.Precision.HIGHEST, preferred_element_type=F32)
    out_ref[...] = summed / jnp.maximum(coverage_ref[...], 1.0)


def filter_rows(sky, coverage, row_taps, col_taps):
    vmem = pl.BlockSpec(memory_space=pltpu.VMEM)
    return pl.pallas_call(
        filter_kernel,
        out_shape=jax.ShapeDtypeStruct((ROWS, PIX), F32),
        in_specs=[vmem] * 4,
        out_specs=vmem,
        compiler_params=pltpu.CompilerParams(vmem_limit_bytes=32 * 1024 * 1024),
        name="filter",
    )(sky, coverage, row_taps, col_taps)


def routes(tiles, exps):
    east, west, border = [], [], []
    for t in range(tiles):
        for e in range(exps):
            if t % GW < GW - 1:
                east.append((t * exps + e, (t + 1) * exps + e))
            if t % GW > 0:
                west.append((t * exps + e, (t - 1) * exps + e))
        if t >= GW:
            border.append((t * exps, (t - GW) * exps + exps - 1))
        if t < tiles - GW:
            border.append((t * exps + exps - 1, (t + GW) * exps))
    return east, west, border


def send(values, route):
    return lax.ppermute(values, ("tile", "exp"), route)


def rising(taps):
    return jnp.pad(taps, ((0, (-taps.shape[0]) % 4), (0, 256 - KW)))


def falling(taps):
    return jnp.roll(jnp.pad(taps[:, ::-1], ((0, (-taps.shape[0]) % 4), (0, 256 - KW))), 1 - KW, 1)


def shards(template, exposures, masks, basis_rows, basis_cols, psf_row, psf_col):
    east, west, border = routes(lax.axis_size("tile"), lax.axis_size("exp"))
    place = lax.axis_index("exp")
    first_place, last_place = place == 0, place == lax.axis_size("exp") - 1

    coverage = lax.psum_scatter(
        jnp.sum(masks[0], axis=0).astype(F32), "exp", scatter_dimension=0, tiled=True
    )

    own = template[0]
    from_west = send(own[:, -HW:], east)
    from_east = send(own[:, :HW], west)
    wide = jnp.concatenate([from_west, own, from_east], 1)
    from_border = send(jnp.where(first_place, wide[:HW], wide[-HW:]), border)
    block = jnp.pad(jnp.concatenate([wide, from_border], 0), ((0, 6), (0, 108)))
    sky = lax.all_gather(block, "exp", axis=0)

    rounded = lambda taps: taps.astype(BF16).astype(F32)
    parts = fit(
        sky, exposures[0], masks[0], rising(rounded(basis_rows)), falling(rounded(basis_cols))
    )
    swapped = lax.all_to_all(parts, "exp", 0, 0)
    summed = jnp.sum(swapped[:, :84].astype(F32), axis=0)
    from_west = send(summed[:, -HW:], east)
    from_east = send(summed[:, :HW], west)
    wide = jnp.concatenate([from_west, summed, from_east], 1)
    from_border = send(jnp.where(first_place, wide[HW:2 * HW], wide[ROWS:ROWS + HW]), border)
    zeros = jnp.zeros_like(from_border)
    wide = jnp.concatenate(
        [
            jnp.where(first_place, from_border, wide[:HW]),
            wide[HW:HW + ROWS],
            jnp.where(last_place, from_border, wide[HW + ROWS:]),
        ],
        0,
    )
    wide = jnp.pad(wide, ((0, 4), (0, 108)))
    return filter_rows(wide, coverage, rising(psf_row[None])[:1], falling(psf_col[None])[:1])[None]


def solution(mesh):
    placed = (
        P("tile", "exp", None),
        P("tile", "exp", None, None),
        P("tile", "exp", None, None),
        P(),
        P(),
        P(),
        P(),
    )
    return jax.shard_map(
        shards, mesh=mesh, in_specs=placed, out_specs=P("tile", "exp", None), check_vma=False
    )
```

```python
import jax
import jax.numpy as jnp
from jax import lax
from jax.experimental import pallas as pl
from jax.experimental.pallas import tpu as pltpu
from jax.sharding import PartitionSpec as P

HW = 10
KW = 21
NB = 27
GW = 8
PIX = 256
ROWS = 64
SLAB = 32
PITCH = PIX + 8
F32 = jnp.float32
BF16 = jnp.bfloat16


def toeplitz_rows(taps, rows):
    return pltpu.roll(jnp.broadcast_to(taps, (rows, taps.shape[1])), 0, 1, stride=1, stride_axis=0)


def fit_kernel(
    sky_ref, images_ref, masks_ref, row_taps_ref, col_taps_ref, out_ref,
    window, col_band, row_band, first, slab_wide, slab, plane, counts,
):
    pieces = [sky_ref[k].astype(F32) for k in range(4)]
    window[...] = jnp.concatenate(
        [pieces[0][ROWS:ROWS + HW]] + [piece[:ROWS] for piece in pieces]
        + [pieces[3][ROWS:ROWS + HW], jnp.zeros((12, 384), F32)], 0
    ).astype(BF16)

    def build(b, carry):
        col = toeplitz_rows(col_taps_ref[pl.ds(b, 1), :], 256)
        col_band[b // 2, :, pl.ds(pl.multiple_of((b % 2) * 128, 128), 128)] = col[:, :128].astype(BF16)
        row_band[b] = toeplitz_rows(row_taps_ref[pl.ds(b, 1), :], 128).astype(BF16)
        return carry

    lax.fori_loop(0, NB + 1, build, 0, unroll=4)

    def columns(pair, carry):
        for half in range(2):
            out = jnp.dot(
                window[:, half * 128:half * 128 + 256], col_band[pair], preferred_element_type=F32
            ).astype(BF16)
            first[2 * pair, :, half * 128:half * 128 + 128] = out[:, :128]
            first[2 * pair + 1, :, half * 128:half * 128 + 128] = out[:, 128:]
        return carry

    lax.fori_loop(0, (NB + 1) // 2, columns, 0, unroll=7)

    for k in range(4):
        for half in range(2):
            slab_wide[half, pl.ds((NB + k) * PITCH, PIX), :] = images_ref[
                k, :, half * 128:half * 128 + 128
            ].astype(F32)
    for half in range(2):
        slab_wide[half, pl.ds((SLAB - 1) * PITCH, PIX), :] = jnp.zeros((PIX, 128), F32)

    def rows_pass(b, carry):
        for block in range(2):
            out = jnp.dot(
                row_band[b, :, :160], first[b, block * 128:block * 128 + 160, :],
                preferred_element_type=F32,
            )
            for half in range(2):
                slab_wide[half, pl.ds(pl.multiple_of(b * PITCH + block * 128, 8), 128), :] = out[
                    :, half * 128:half * 128 + 128
                ]
        return carry

    lax.fori_loop(0, NB, rows_pass, 0, unroll=9)

    def gram(group, total):
        base = pl.multiple_of(group * 8 * SLAB, 8 * SLAB)
        at = pl.multiple_of(group * 8, 8)
        valid = [masks_ref[k, pl.ds(at, 8), :].astype(F32) for k in range(4)]
        for i in range(8):
            here = pl.ds(base + i * SLAB, SLAB)
            there = pl.ds(group * 8 + i, SLAB, stride=PITCH)
            rows = jnp.concatenate([slab_wide[0, there, :], slab_wide[1, there, :]], 1)
            low = rows.astype(BF16)
            slab[here, :] = low
            masked = jnp.concatenate(
                [low * jnp.broadcast_to(v[i:i + 1].astype(BF16), low.shape) for v in valid], 0
            )
            total = total + lax.dot_general(
                low, masked, (((1,), (1,)), ((), ())), preferred_element_type=F32
            )
        return total

    matrix = lax.fori_loop(0, PIX // 8, gram, jnp.zeros((SLAB, 4 * SLAB), F32), unroll=2)

    lane = lax.broadcasted_iota(jnp.int32, (SLAB, 4 * SLAB), 1)
    row = lax.broadcasted_iota(jnp.int32, (SLAB, 4 * SLAB), 0)
    of_exposure = lane // SLAB
    of_basis = lane % SLAB
    for k in range(NB):
        column = jnp.take_along_axis(matrix, of_exposure * SLAB + k, axis=1)
        pivot_row = matrix[k:k + 1, :]
        pivot = column[k:k + 1, :]
        scaled = jnp.where(of_basis[:1] == k, 0.0, pivot_row / pivot)
        matrix = matrix - column * scaled
    top = jnp.sum(jnp.where(row == NB + of_exposure, matrix, 0.0), axis=0, keepdims=True)
    bottom = jnp.sum(jnp.where(row == of_basis, matrix, 0.0), axis=0, keepdims=True)
    solved = jnp.broadcast_to(top / bottom, (8, 4 * SLAB))
    lane8 = lax.broadcasted_iota(jnp.int32, (8, 4 * SLAB), 1)
    row8 = lax.broadcasted_iota(jnp.int32, (8, 4 * SLAB), 0)
    weights = []
    for k in range(4):
        own = -jnp.take_along_axis(solved, lane8 % SLAB + k * SLAB, axis=1)
        own = jnp.where(lane8 % SLAB == NB + k, 1.0, jnp.where(lane8 % SLAB >= NB, 0.0, own))
        weights.append(
            jnp.concatenate([jnp.where(row8 == lane8 // SLAB + 4 * half, own, 0.0) for half in range(2)], 1)
        )
    weights = jnp.concatenate(weights, 0).astype(BF16)

    plane[...] = jnp.zeros_like(plane)

    def residual(group, carry):
        base = pl.multiple_of(group * 8 * SLAB, 8 * SLAB)
        at = pl.multiple_of(group * 8, 8)
        left = jnp.dot(weights, slab[pl.ds(base, 8 * SLAB), :], preferred_element_type=F32)
        total = jnp.zeros((8, PIX), F32)
        seen = jnp.zeros((8, PIX), F32)
        for k in range(4):
            valid = masks_ref[k, pl.ds(at, 8), :].astype(F32)
            seen = seen + valid
            total = total + (valid * left[8 * k:8 * k + 8]).astype(BF16).astype(F32)
        plane[pl.ds(pl.multiple_of(group * 8 + 16, 8), 8), :] = total
        counts[pl.ds(at, 8), :] = seen
        return carry

    lax.fori_loop(0, PIX // 8, residual, 0, unroll=4)
    for k in range(4):
        out_ref[k] = jnp.concatenate(
            [counts[64 * k:64 * k + 64, :], plane[64 * k + 6:64 * k + 6 + 96, :]], 0
        ).astype(BF16)


def fit(sky, images, masks, row_taps, col_taps):
    vmem = pl.BlockSpec(memory_space=pltpu.VMEM)
    return pl.pallas_call(
        fit_kernel,
        out_shape=jax.ShapeDtypeStruct((4, 160, PIX), BF16),
        in_specs=[vmem] * 5,
        out_specs=vmem,
        scratch_shapes=[
            pltpu.VMEM((288, 384), BF16),
            pltpu.VMEM((14, 256, 256), BF16),
            pltpu.VMEM((28, 128, 256), BF16),
            pltpu.VMEM((28, 288, 256), BF16),
            pltpu.VMEM((2, PITCH * SLAB, 128), F32),
            pltpu.VMEM((PIX * SLAB, 256), BF16),
            pltpu.VMEM((320, PIX), F32),
            pltpu.VMEM((PIX, PIX), F32),
        ],
        compiler_params=pltpu.CompilerParams(vmem_limit_bytes=48 * 1024 * 1024),
        name="fit",
    )(sky, images, masks, row_taps, col_taps)


def filter_kernel(sky_ref, coverage_ref, row_taps_ref, col_taps_ref, out_ref):
    col_band = toeplitz_rows(col_taps_ref[...], 256)[:, :128]
    row_band = toeplitz_rows(row_taps_ref[...], ROWS)[:, :88]
    halves = [
        jnp.dot(sky_ref[:, half * 128:half * 128 + 256], col_band, precision=lax.Precision.HIGHEST,
                preferred_element_type=F32)
        for half in range(2)
    ]
    column_pass = jnp.concatenate(halves, 1)
    summed = jnp.dot(row_band, column_pass, precision=lax.Precision.HIGHEST, preferred_element_type=F32)
    out_ref[...] = summed / jnp.maximum(coverage_ref[...], 1.0)


def filter_rows(sky, coverage, row_taps, col_taps):
    vmem = pl.BlockSpec(memory_space=pltpu.VMEM)
    return pl.pallas_call(
        filter_kernel,
        out_shape=jax.ShapeDtypeStruct((ROWS, PIX), F32),
        in_specs=[vmem] * 4,
        out_specs=vmem,
        compiler_params=pltpu.CompilerParams(vmem_limit_bytes=32 * 1024 * 1024),
        name="filter",
    )(sky, coverage, row_taps, col_taps)


def routes(tiles, exps):
    east, west, border = [], [], []
    for t in range(tiles):
        for e in range(exps):
            if t % GW < GW - 1:
                east.append((t * exps + e, (t + 1) * exps + e))
            if t % GW > 0:
                west.append((t * exps + e, (t - 1) * exps + e))
        if t >= GW:
            border.append((t * exps, (t - GW) * exps + exps - 1))
        if t < tiles - GW:
            border.append((t * exps + exps - 1, (t + GW) * exps))
    return east, west, border


def send(values, route):
    return lax.ppermute(values, ("tile", "exp"), route)


def rising(taps):
    return jnp.pad(taps, ((0, (-taps.shape[0]) % 4), (0, 256 - KW)))


def falling(taps):
    return jnp.roll(jnp.pad(taps[:, ::-1], ((0, (-taps.shape[0]) % 4), (0, 256 - KW))), 1 - KW, 1)


def shards(template, exposures, masks, basis_rows, basis_cols, psf_row, psf_col):
    east, west, border = routes(lax.axis_size("tile"), lax.axis_size("exp"))
    place = lax.axis_index("exp")
    first_place, last_place = place == 0, place == lax.axis_size("exp") - 1

    own = template[0]
    from_west = send(own[:, -HW:], east)
    from_east = send(own[:, :HW], west)
    wide = lax.optimization_barrier(jnp.concatenate([from_west, own, from_east], 1))
    from_border = send(jnp.where(first_place, wide[:HW], wide[-HW:]), border)
    block = jnp.pad(jnp.concatenate([wide, from_border], 0), ((0, 6), (0, 108)))
    sky = lax.all_gather(block, "exp", axis=0)

    rounded = lambda taps: taps.astype(BF16).astype(F32)
    parts = fit(
        sky, exposures[0], masks[0], rising(rounded(basis_rows)), falling(rounded(basis_cols))
    )
    swapped = lax.all_to_all(parts, "exp", 0, 0)
    coverage = jnp.sum(swapped[:, :ROWS].astype(F32), axis=0)
    summed = jnp.sum(swapped[:, ROWS:ROWS + 84].astype(F32), axis=0)
    from_west = send(summed[:, -HW:], east)
    from_east = send(summed[:, :HW], west)
    wide = jnp.concatenate([from_west, summed, from_east], 1)
    from_border = send(jnp.where(first_place, wide[HW:2 * HW], wide[ROWS:ROWS + HW]), border)
    zeros = jnp.zeros_like(from_border)
    wide = jnp.concatenate(
        [
            jnp.where(first_place, from_border, wide[:HW]),
            wide[HW:HW + ROWS],
            jnp.where(last_place, from_border, wide[HW + ROWS:]),
        ],
        0,
    )
    wide = jnp.pad(wide, ((0, 4), (0, 108)))
    return filter_rows(wide, coverage, rising(psf_row[None])[:1], falling(psf_col[None])[:1])[None]


def solution(mesh):
    placed = (
        P("tile", "exp", None),
        P("tile", "exp", None, None),
        P("tile", "exp", None, None),
        P(),
        P(),
        P(),
        P(),
    )
    return jax.shard_map(
        shards, mesh=mesh, in_specs=placed, out_specs=P("tile", "exp", None), check_vma=False
    )
```

```python
import jax
import jax.numpy as jnp
from jax import lax
from jax.experimental import pallas as pl
from jax.experimental.pallas import tpu as pltpu
from jax.sharding import PartitionSpec as P

HW = 10
KW = 21
NB = 27
GW = 8
PIX = 256
ROWS = 64
SLAB = 32
PITCH = PIX + 8
F32 = jnp.float32
BF16 = jnp.bfloat16


def toeplitz_rows(taps, rows):
    return pltpu.roll(jnp.broadcast_to(taps, (rows, taps.shape[1])), 0, 1, stride=1, stride_axis=0)


def fit_kernel(
    place_ref, sky_any, images_ref, masks_ref, row_taps_ref, col_taps_ref, mine_ref, theirs_ref,
    sky_ref, window, col_band, row_band, first, slab_wide, slab, plane, counts, sky_sem,
):
    sky_copy = pltpu.make_async_copy(sky_any, sky_ref, sky_sem)
    sky_copy.start()

    def build(b, carry):
        col = toeplitz_rows(col_taps_ref[pl.ds(b, 1), :], 256)
        col_band[b // 2, :, pl.ds(pl.multiple_of((b % 2) * 128, 128), 128)] = col[:, :128].astype(BF16)
        row_band[b] = toeplitz_rows(row_taps_ref[pl.ds(b, 1), :], 128).astype(BF16)
        return carry

    lax.fori_loop(0, NB + 1, build, 0, unroll=4)

    sky_copy.wait()
    pieces = [sky_ref[k].astype(F32) for k in range(4)]
    window[...] = jnp.concatenate(
        [pieces[0][ROWS:ROWS + HW]] + [piece[:ROWS] for piece in pieces]
        + [pieces[3][ROWS:ROWS + HW], jnp.zeros((12, 384), F32)], 0
    ).astype(BF16)

    def columns(pair, carry):
        for half in range(2):
            out = jnp.dot(
                window[:, half * 128:half * 128 + 256], col_band[pair], preferred_element_type=F32
            ).astype(BF16)
            first[2 * pair, :, half * 128:half * 128 + 128] = out[:, :128]
            first[2 * pair + 1, :, half * 128:half * 128 + 128] = out[:, 128:]
        return carry

    lax.fori_loop(0, (NB + 1) // 2, columns, 0, unroll=7)

    for k in range(4):
        for half in range(2):
            slab_wide[half, pl.ds((NB + k) * PITCH, PIX), :] = images_ref[
                k, :, half * 128:half * 128 + 128
            ].astype(F32)
    for half in range(2):
        slab_wide[half, pl.ds((SLAB - 1) * PITCH, PIX), :] = jnp.zeros((PIX, 128), F32)

    def rows_pass(b, carry):
        for block in range(2):
            out = jnp.dot(
                row_band[b, :, :160], first[b, block * 128:block * 128 + 160, :],
                preferred_element_type=F32,
            )
            for half in range(2):
                slab_wide[half, pl.ds(pl.multiple_of(b * PITCH + block * 128, 8), 128), :] = out[
                    :, half * 128:half * 128 + 128
                ]
        return carry

    lax.fori_loop(0, NB, rows_pass, 0, unroll=9)

    def gram(group, total):
        base = pl.multiple_of(group * 8 * SLAB, 8 * SLAB)
        at = pl.multiple_of(group * 8, 8)
        valid = [masks_ref[k, pl.ds(at, 8), :].astype(F32) for k in range(4)]
        for i in range(8):
            here = pl.ds(base + i * SLAB, SLAB)
            there = pl.ds(group * 8 + i, SLAB, stride=PITCH)
            rows = jnp.concatenate([slab_wide[0, there, :], slab_wide[1, there, :]], 1)
            low = rows.astype(BF16)
            slab[here, :] = low
            masked = jnp.concatenate(
                [low * jnp.broadcast_to(v[i:i + 1].astype(BF16), low.shape) for v in valid], 0
            )
            total = total + lax.dot_general(
                low, masked, (((1,), (1,)), ((), ())), preferred_element_type=F32
            )
        return total

    matrix = lax.fori_loop(0, PIX // 8, gram, jnp.zeros((SLAB, 4 * SLAB), F32), unroll=2)

    lane = lax.broadcasted_iota(jnp.int32, (SLAB, 4 * SLAB), 1)
    row = lax.broadcasted_iota(jnp.int32, (SLAB, 4 * SLAB), 0)
    of_exposure = lane // SLAB
    of_basis = lane % SLAB
    for k in range(NB):
        column = jnp.take_along_axis(matrix, of_exposure * SLAB + k, axis=1)
        pivot_row = matrix[k:k + 1, :]
        pivot = column[k:k + 1, :]
        scaled = jnp.where(of_basis[:1] == k, 0.0, pivot_row / pivot)
        matrix = matrix - column * scaled
    top = jnp.sum(jnp.where(row == NB + of_exposure, matrix, 0.0), axis=0, keepdims=True)
    bottom = jnp.sum(jnp.where(row == of_basis, matrix, 0.0), axis=0, keepdims=True)
    solved = jnp.broadcast_to(top / bottom, (8, 4 * SLAB))
    lane8 = lax.broadcasted_iota(jnp.int32, (8, 4 * SLAB), 1)
    row8 = lax.broadcasted_iota(jnp.int32, (8, 4 * SLAB), 0)
    weights = []
    for k in range(4):
        own = -jnp.take_along_axis(solved, lane8 % SLAB + k * SLAB, axis=1)
        own = jnp.where(lane8 % SLAB == NB + k, 1.0, jnp.where(lane8 % SLAB >= NB, 0.0, own))
        weights.append(
            jnp.concatenate([jnp.where(row8 == lane8 // SLAB + 4 * half, own, 0.0) for half in range(2)], 1)
        )
    weights = jnp.concatenate(weights, 0).astype(BF16)

    plane[...] = jnp.zeros_like(plane)

    def residual(group, carry):
        base = pl.multiple_of(group * 8 * SLAB, 8 * SLAB)
        at = pl.multiple_of(group * 8, 8)
        left = jnp.dot(weights, slab[pl.ds(base, 8 * SLAB), :], preferred_element_type=F32)
        total = jnp.zeros((8, PIX), F32)
        seen = jnp.zeros((8, PIX), F32)
        for k in range(4):
            valid = masks_ref[k, pl.ds(at, 8), :].astype(F32)
            seen = seen + valid
            total = total + (valid * left[8 * k:8 * k + 8]).astype(BF16).astype(F32)
        plane[pl.ds(pl.multiple_of(group * 8 + 16, 8), 8), :] = total
        counts[pl.ds(at, 8), :] = seen
        return carry

    lax.fori_loop(0, PIX // 8, residual, 0, unroll=4)

    def block(k):
        return jnp.concatenate(
            [counts[ROWS * k:ROWS * k + ROWS, :], plane[ROWS * k + 6:ROWS * k + 6 + 88, :]], 0
        ).astype(BF16)

    for k in range(4):

        @pl.when(place_ref[0] == k)
        def _():
            mine_ref[0], mine_ref[1] = block(k), block(k ^ 2)
            theirs_ref[0], theirs_ref[1] = block(k ^ 1), block(k ^ 3)


def fit(place, sky, images, masks, row_taps, col_taps):
    vmem = pl.BlockSpec(memory_space=pltpu.VMEM)
    return pl.pallas_call(
        fit_kernel,
        out_shape=[jax.ShapeDtypeStruct((2, 152, PIX), BF16)] * 2,
        in_specs=[pl.BlockSpec(memory_space=pltpu.SMEM), pl.BlockSpec(memory_space=pl.ANY)] + [vmem] * 4,
        out_specs=[vmem] * 2,
        scratch_shapes=[
            pltpu.VMEM((4, 80, 384), BF16),
            pltpu.VMEM((288, 384), BF16),
            pltpu.VMEM((14, 256, 256), BF16),
            pltpu.VMEM((28, 128, 256), BF16),
            pltpu.VMEM((28, 288, 256), BF16),
            pltpu.VMEM((2, PITCH * SLAB, 128), F32),
            pltpu.VMEM((PIX * SLAB, 256), BF16),
            pltpu.VMEM((320, PIX), F32),
            pltpu.VMEM((PIX, PIX), F32),
            pltpu.SemaphoreType.DMA(()),
        ],
        compiler_params=pltpu.CompilerParams(vmem_limit_bytes=48 * 1024 * 1024),
        name="fit",
    )(place, sky, images, masks, row_taps, col_taps)


def filter_kernel(sky_ref, coverage_ref, row_taps_ref, col_taps_ref, out_ref):
    col_band = toeplitz_rows(col_taps_ref[...], 256)[:, :128]
    row_band = toeplitz_rows(row_taps_ref[...], ROWS)[:, :88]
    halves = [
        jnp.dot(sky_ref[:, half * 128:half * 128 + 256], col_band, precision=lax.Precision.HIGHEST,
                preferred_element_type=F32)
        for half in range(2)
    ]
    column_pass = jnp.concatenate(halves, 1)
    summed = jnp.dot(row_band, column_pass, precision=lax.Precision.HIGHEST, preferred_element_type=F32)
    out_ref[...] = summed / jnp.maximum(coverage_ref[...], 1.0)


def filter_rows(sky, coverage, row_taps, col_taps):
    vmem = pl.BlockSpec(memory_space=pltpu.VMEM)
    return pl.pallas_call(
        filter_kernel,
        out_shape=jax.ShapeDtypeStruct((ROWS, PIX), F32),
        in_specs=[vmem] * 4,
        out_specs=vmem,
        compiler_params=pltpu.CompilerParams(vmem_limit_bytes=32 * 1024 * 1024),
        name="filter",
    )(sky, coverage, row_taps, col_taps)


def routes(tiles, exps):
    east, west, border, core, half = [], [], [], [], []
    for t in range(tiles):
        for e in range(exps):
            core.append((t * exps + e, t * exps + (e ^ 1)))
            half.append((t * exps + e, t * exps + (e ^ 2)))
            if t % GW < GW - 1:
                east.append((t * exps + e, (t + 1) * exps + e))
            if t % GW > 0:
                west.append((t * exps + e, (t - 1) * exps + e))
        if t >= GW:
            border.append((t * exps, (t - GW) * exps + exps - 1))
        if t < tiles - GW:
            border.append((t * exps + exps - 1, (t + GW) * exps))
    return east, west, border, core, half


def send(values, route):
    return lax.ppermute(values, ("tile", "exp"), route)


def rising(taps):
    return jnp.pad(taps, ((0, (-taps.shape[0]) % 4), (0, 256 - KW)))


def falling(taps):
    return jnp.roll(jnp.pad(taps[:, ::-1], ((0, (-taps.shape[0]) % 4), (0, 256 - KW))), 1 - KW, 1)


def shards(template, exposures, masks, basis_rows, basis_cols, psf_row, psf_col):
    east, west, border, core, half = routes(lax.axis_size("tile"), lax.axis_size("exp"))
    place = lax.axis_index("exp")
    first_place, last_place = place == 0, place == lax.axis_size("exp") - 1

    own = template[0]
    from_west = send(own, east)[:, -HW:]
    from_east = send(own, west)[:, :HW]
    wide = lax.optimization_barrier(jnp.concatenate([from_west, own, from_east], 1))
    from_border = send(jnp.where(first_place, wide[:HW], wide[-HW:]), border)
    block = jnp.pad(jnp.concatenate([wide, from_border], 0), ((0, 6), (0, 108)))
    sky = lax.all_gather(block, "exp", axis=0)

    rounded = lambda taps: taps.astype(BF16).astype(F32)
    mine, theirs = fit(
        place[None], sky, exposures[0], masks[0], rising(rounded(basis_rows)), falling(rounded(basis_cols))
    )
    pair = mine.astype(F32) + send(theirs, core).astype(F32)
    whole = pair[0] + send(pair[1].astype(BF16), half).astype(F32)
    coverage, summed = whole[:ROWS], whole[ROWS:ROWS + 84]
    from_west = send(summed[:, -HW:], east)
    from_east = send(summed[:, :HW], west)
    wide = jnp.concatenate([from_west, summed, from_east], 1)
    from_border = send(jnp.where(first_place, wide[HW:2 * HW], wide[ROWS:ROWS + HW]), border)
    zeros = jnp.zeros_like(from_border)
    wide = jnp.concatenate(
        [
            jnp.where(first_place, from_border, wide[:HW]),
            wide[HW:HW + ROWS],
            jnp.where(last_place, from_border, wide[HW + ROWS:]),
        ],
        0,
    )
    wide = jnp.pad(wide, ((0, 4), (0, 108)))
    return filter_rows(wide, coverage, rising(psf_row[None])[:1], falling(psf_col[None])[:1])[None]


def solution(mesh):
    placed = (
        P("tile", "exp", None),
        P("tile", "exp", None, None),
        P("tile", "exp", None, None),
        P(),
        P(),
        P(),
        P(),
    )
    return jax.shard_map(
        shards, mesh=mesh, in_specs=placed, out_specs=P("tile", "exp", None), check_vma=False
    )
```

```python
import jax
import jax.numpy as jnp
from jax import lax
from jax.experimental import pallas as pl
from jax.experimental.pallas import tpu as pltpu
from jax.sharding import PartitionSpec as P

HW = 10
KW = 21
NB = 27
GW = 8
PIX = 256
ROWS = 64
HALF = 128
SLAB = 32
PITCH = PIX + 8
F32 = jnp.float32
BF16 = jnp.bfloat16


def toeplitz_rows(taps, rows):
    return pltpu.roll(jnp.broadcast_to(taps, (rows, taps.shape[1])), 0, 1, stride=1, stride_axis=0)


def fit_kernel(
    place_ref, own_any, far_any, far_core_any, edge_any, edge_core_any, images_ref, masks_ref, row_taps_ref, col_taps_ref, mine_ref, theirs_ref,
    own_ref, far_ref, edge_ref, window, col_band, row_band, first, slab_wide, slab, plane, counts, sky_sem,
):
    arriving = [
        pltpu.make_async_copy(source, target, sky_sem.at[k])
        for k, (source, target) in enumerate((
            (own_any, own_ref), (far_any, far_ref.at[0]), (far_core_any, far_ref.at[1]),
            (edge_any, edge_ref.at[0]), (edge_core_any, edge_ref.at[1]),
        ))
    ]
    for copy in arriving:
        copy.start()

    def build(b, carry):
        col = toeplitz_rows(col_taps_ref[pl.ds(b, 1), :], 256)
        col_band[b // 2, :, pl.ds(pl.multiple_of((b % 2) * 128, 128), 128)] = col[:, :128].astype(BF16)
        row_band[b] = toeplitz_rows(row_taps_ref[pl.ds(b, 1), :], 128).astype(BF16)
        return carry

    lax.fori_loop(0, NB + 1, build, 0, unroll=14)

    for copy in arriving:
        copy.wait()
    on_left, on_top = place_ref[0] % 2 == 0, place_ref[0] < 2
    own = own_ref[...].astype(F32)
    quarters = [far_ref[k].astype(F32) for k in range(2)]
    edges = [edge_ref[k].astype(F32) for k in range(2)]
    far = jnp.concatenate([jnp.where(on_left, *quarters), jnp.where(on_left, *quarters[::-1])], 0)
    north, south = jnp.where(on_left, *edges), jnp.where(on_left, *edges[::-1])
    window[...] = jnp.concatenate(
        [north[16 - HW:], jnp.where(on_top, own, far), jnp.where(on_top, far, own), south[:HW],
         jnp.zeros((12, 384), F32)], 0
    ).astype(BF16)

    def columns(pair, carry):
        for half in range(2):
            out = jnp.dot(
                window[:, half * 128:half * 128 + 256], col_band[pair], preferred_element_type=F32
            ).astype(BF16)
            first[2 * pair, :, half * 128:half * 128 + 128] = out[:, :128]
            first[2 * pair + 1, :, half * 128:half * 128 + 128] = out[:, 128:]
        return carry

    lax.fori_loop(0, (NB + 1) // 2, columns, 0, unroll=14)

    for k in range(4):
        for half in range(2):
            slab_wide[half, pl.ds((NB + k) * PITCH, PIX), :] = images_ref[
                k, :, half * 128:half * 128 + 128
            ].astype(F32)
    for half in range(2):
        slab_wide[half, pl.ds((SLAB - 1) * PITCH, PIX), :] = jnp.zeros((PIX, 128), F32)

    def rows_pass(b, carry):
        for block in range(2):
            out = jnp.dot(
                row_band[b, :, :160], first[b, block * 128:block * 128 + 160, :],
                preferred_element_type=F32,
            )
            for half in range(2):
                slab_wide[half, pl.ds(pl.multiple_of(b * PITCH + block * 128, 8), 128), :] = out[
                    :, half * 128:half * 128 + 128
                ]
        return carry

    lax.fori_loop(0, NB, rows_pass, 0, unroll=27)

    def gram(group, total):
        base = pl.multiple_of(group * 8 * SLAB, 8 * SLAB)
        at = pl.multiple_of(group * 8, 8)
        valid = [masks_ref[k, pl.ds(at, 8), :].astype(F32) for k in range(4)]
        for i in range(8):
            here = pl.ds(base + i * SLAB, SLAB)
            there = pl.ds(group * 8 + i, SLAB, stride=PITCH)
            rows = jnp.concatenate([slab_wide[0, there, :], slab_wide[1, there, :]], 1)
            low = rows.astype(BF16)
            slab[here, :] = low
            masked = jnp.concatenate(
                [low * jnp.broadcast_to(v[i:i + 1].astype(BF16), low.shape) for v in valid], 0
            )
            total = total + lax.dot_general(
                low, masked, (((1,), (1,)), ((), ())), preferred_element_type=F32
            )
        return total

    matrix = lax.fori_loop(0, PIX // 8, gram, jnp.zeros((SLAB, 4 * SLAB), F32), unroll=2)

    lane = lax.broadcasted_iota(jnp.int32, (SLAB, 4 * SLAB), 1)
    row = lax.broadcasted_iota(jnp.int32, (SLAB, 4 * SLAB), 0)
    of_exposure = lane // SLAB
    of_basis = lane % SLAB
    for k in range(NB):
        column = jnp.take_along_axis(matrix, of_exposure * SLAB + k, axis=1)
        pivot_row = matrix[k:k + 1, :]
        pivot = column[k:k + 1, :]
        scaled = jnp.where(of_basis[:1] == k, 0.0, pivot_row / pivot)
        matrix = matrix - column * scaled
    top = jnp.sum(jnp.where(row == NB + of_exposure, matrix, 0.0), axis=0, keepdims=True)
    bottom = jnp.sum(jnp.where(row == of_basis, matrix, 0.0), axis=0, keepdims=True)
    solved = jnp.broadcast_to(top / bottom, (8, 4 * SLAB))
    lane8 = lax.broadcasted_iota(jnp.int32, (8, 4 * SLAB), 1)
    row8 = lax.broadcasted_iota(jnp.int32, (8, 4 * SLAB), 0)
    weights = []
    for k in range(4):
        own = -jnp.take_along_axis(solved, lane8 % SLAB + k * SLAB, axis=1)
        own = jnp.where(lane8 % SLAB == NB + k, 1.0, jnp.where(lane8 % SLAB >= NB, 0.0, own))
        weights.append(
            jnp.concatenate([jnp.where(row8 == lane8 // SLAB + 4 * half, own, 0.0) for half in range(2)], 1)
        )
    weights = jnp.concatenate(weights, 0).astype(BF16)

    plane[...] = jnp.zeros_like(plane)

    def residual(group, carry):
        base = pl.multiple_of(group * 8 * SLAB, 8 * SLAB)
        at = pl.multiple_of(group * 8, 8)
        left = jnp.dot(weights, slab[pl.ds(base, 8 * SLAB), :], preferred_element_type=F32)
        total = jnp.zeros((8, PIX), F32)
        seen = jnp.zeros((8, PIX), F32)
        for k in range(4):
            valid = masks_ref[k, pl.ds(at, 8), :].astype(F32)
            seen = seen + valid
            total = total + (valid * left[8 * k:8 * k + 8]).astype(BF16).astype(F32)
        plane[pl.ds(pl.multiple_of(group * 8 + 16, 8), 8), :] = total
        counts[pl.ds(at, 8), :] = seen
        return carry

    lax.fori_loop(0, PIX // 8, residual, 0, unroll=8)

    def block(k):
        side = pl.ds(HALF * (k % 2), HALF)
        return jnp.concatenate(
            [
                plane[16 + 118 * (k // 2):16 + 118 * (k // 2) + HALF + 16, side],
                jnp.concatenate(
                    [counts[ROWS * k:ROWS * k + ROWS, :HALF], counts[ROWS * k:ROWS * k + ROWS, HALF:],
                     jnp.zeros((16, HALF), F32)], 0
                ),
            ],
            1,
        ).astype(BF16)

    for k in range(4):

        @pl.when(place_ref[0] == k)
        def _():
            mine_ref[0], mine_ref[1] = block(k), block(k ^ 2)
            theirs_ref[0], theirs_ref[1] = block(k ^ 1), block(k ^ 3)


def fit(place, skies, images, masks, row_taps, col_taps):
    vmem = pl.BlockSpec(memory_space=pltpu.VMEM)
    return pl.pallas_call(
        fit_kernel,
        out_shape=[jax.ShapeDtypeStruct((2, HALF + 16, PIX), BF16)] * 2,
        in_specs=[pl.BlockSpec(memory_space=pltpu.SMEM), *[pl.BlockSpec(memory_space=pl.ANY)] * 5] + [vmem] * 4,
        out_specs=[vmem] * 2,
        scratch_shapes=[
            pltpu.VMEM((HALF, 384), BF16),
            pltpu.VMEM((2, ROWS, 384), BF16),
            pltpu.VMEM((2, 16, 384), BF16),
            pltpu.VMEM((288, 384), BF16),
            pltpu.VMEM((14, 256, 256), BF16),
            pltpu.VMEM((28, 128, 256), BF16),
            pltpu.VMEM((28, 288, 256), BF16),
            pltpu.VMEM((2, PITCH * (SLAB + 1), 128), F32),
            pltpu.VMEM((PIX * SLAB, 256), BF16),
            pltpu.VMEM((320, PIX), F32),
            pltpu.VMEM((PIX, PIX), F32),
            pltpu.SemaphoreType.DMA((5,)),
        ],
        compiler_params=pltpu.CompilerParams(vmem_limit_bytes=48 * 1024 * 1024),
        name="fit",
    )(place, *skies, images, masks, row_taps, col_taps)


def filter_kernel(
    place_ref, near_ref, far_ref, beside_ref, edge_ref, edge_too_ref, row_taps_ref, col_taps_ref,
    keep_ref, give_ref, seen_ref,
):
    on_left, on_top = place_ref[0] % 2 == 0, place_ref[0] < 2
    far = far_ref[...].astype(F32)
    total = near_ref[...] + far[:, :PIX]
    seen = jnp.maximum(total[:HALF, HALF:], 1.0)
    seen_ref[...] = jnp.concatenate([seen[:ROWS], seen[ROWS:]], 1)
    main = total[:HALF + HW, :HALF]
    beside = beside_ref[0] + far[:HALF + HW, PIX:PIX + HW]
    edge = edge_ref[...] + edge_too_ref[...]
    edge = jnp.where(on_left, jnp.concatenate([edge[:, HALF:], edge[:, :HALF]], 1), edge)
    core = jnp.where(on_left, jnp.concatenate([beside, main], 1), jnp.concatenate([main, beside], 1))
    sky = jnp.where(on_top, jnp.concatenate([edge, core], 0), jnp.concatenate([core, edge], 0))
    sky = jnp.concatenate([sky, jnp.zeros((4, HALF + HW), F32)], 0)
    sky = jnp.concatenate([sky, jnp.zeros((HALF + 24, 6), F32)], 1)
    taps = jnp.where(on_left, col_taps_ref[...], pltpu.roll(col_taps_ref[...], HALF + HW, 1))
    col_band = toeplitz_rows(taps, HALF + 16)
    row_band = toeplitz_rows(row_taps_ref[...], HALF)[:, :HALF + 24]
    column_pass = jnp.dot(sky, col_band, precision=lax.Precision.HIGHEST, preferred_element_type=F32)
    lane = lax.broadcasted_iota(jnp.int32, column_pass.shape, 1)
    reached = jnp.logical_and(lane >= jnp.where(on_left, 0, HALF - HW), lane < jnp.where(on_left, HALF + HW, PIX))
    column_pass = jnp.where(reached, column_pass, 0.0)
    part = jnp.dot(row_band, column_pass, precision=lax.Precision.HIGHEST, preferred_element_type=F32)
    keep_ref[...] = jnp.where(on_left, part[:ROWS], part[ROWS:])
    give_ref[...] = jnp.where(on_left, part[ROWS:], part[:ROWS])


def filter_half(place, *operands):
    vmem = pl.BlockSpec(memory_space=pltpu.VMEM)
    return pl.pallas_call(
        filter_kernel,
        out_shape=[jax.ShapeDtypeStruct((ROWS, PIX), F32)] * 3,
        in_specs=[pl.BlockSpec(memory_space=pltpu.SMEM)] + [vmem] * len(operands),
        out_specs=[vmem] * 3,
        compiler_params=pltpu.CompilerParams(vmem_limit_bytes=32 * 1024 * 1024),
        name="filter",
    )(place, *operands)


def routes(tiles, exps):
    core, chip, beside, border, border_too, edge = [], [], [], [], [], []
    for t in range(tiles):
        row, col = t // GW, t % GW
        for e in range(exps):
            here = t * exps + e
            core.append((here, t * exps + (e ^ 1)))
            chip.append((here, t * exps + (e ^ 2)))
            col_to = col + (1 if e % 2 else -1)
            row_to = row + (1 if e // 2 else -1)
            in_cols, in_rows = 0 <= col_to < GW, 0 <= row_to < tiles // GW
            if in_cols:
                beside.append((here, (row * GW + col_to) * exps + (e ^ 1)))
            if in_rows:
                border.append((here, (row_to * GW + col) * exps + (e ^ 2)))
                border_too.append((t * exps + (e ^ 2), (row_to * GW + col) * exps + (e ^ 2)))
                edge.append((here, (row_to * GW + col) * exps + 2 * (e % 2) + 1 - e // 2))
    return core, chip, beside, border, border_too, edge


def send(values, route):
    return lax.ppermute(values, ("tile", "exp"), route)


def rising(taps):
    return jnp.pad(taps, ((0, (-taps.shape[0]) % 4), (0, 256 - KW)))


def falling(taps):
    return jnp.roll(jnp.pad(taps[:, ::-1], ((0, (-taps.shape[0]) % 4), (0, 256 - KW))), 1 - KW, 1)


def shards(template, exposures, masks, basis_rows, basis_cols, psf_row, psf_col):
    core, chip, beside, border, border_too, edge = routes(lax.axis_size("tile"), lax.axis_size("exp"))
    place = lax.axis_index("exp")
    on_left, on_top = place % 2 == 0, place < 2

    own = template[0]
    other = send(own, core)
    strip = jnp.concatenate(
        [jnp.where(on_left, own[:, :HW], other[:, -HW:]), jnp.where(on_left, other[:, :HW], own[:, -HW:])], 0
    )
    strip = send(strip, beside)
    half = jnp.where(on_left, jnp.concatenate([own, other], 0), jnp.concatenate([other, own], 0))
    strip_core = send(strip, core)
    west, east = jnp.where(on_left, strip, strip_core), jnp.where(on_left, strip_core, strip)
    wide = lax.optimization_barrier(jnp.pad(jnp.concatenate([west, half, east], 1), ((0, 0), (0, 108))))
    far = send(jnp.where(on_left, wide[:ROWS], wide[ROWS:]), chip)
    rows = send(jnp.where(on_top, wide[:16], wide[-16:]), edge)
    far_core, rows_core = send(far, core), send(rows, core)

    rounded = lambda taps: taps.astype(BF16).astype(F32)
    mine, theirs = fit(
        place[None], (wide, far, far_core, rows, rows_core), exposures[0], masks[0],
        rising(rounded(basis_rows)), falling(rounded(basis_cols)),
    )
    pair = mine.astype(F32) + send(theirs, core).astype(F32)
    main = pair[:, :HALF + HW, :HALF]
    strip = send(jnp.where(on_left, main[:, :, :HW], main[:, :, -HW:]), beside)
    far = jnp.concatenate([pair[1], jnp.pad(strip[1], ((0, 6), (0, HALF - HW)))], 1).astype(BF16)
    ends = jnp.concatenate([main, strip], 2)
    far, ends = lax.optimization_barrier((far, ends))
    far = send(far, chip)
    rows = send(jnp.where(on_top, ends[0, :HW], ends[0, -HW:]), border)
    rows_too = send(jnp.where(on_top, ends[1, -HW:], ends[1, :HW]), border_too)
    keep, give, seen = filter_half(
        place[None], pair[0], far, strip, rows, rows_too, rising(psf_row[None])[:1], falling(psf_col[None])[:1]
    )
    return ((keep + send(give, core)) / seen)[None]


def solution(mesh):
    placed = (
        P("tile", "exp", None),
        P("tile", "exp", None, None),
        P("tile", "exp", None, None),
        P(),
        P(),
        P(),
        P(),
    )
    return jax.shard_map(
        shards, mesh=mesh, in_specs=placed, out_specs=P("tile", "exp", None), check_vma=False
    )
```

```python
import jax
import jax.numpy as jnp
from jax import lax
from jax.experimental import pallas as pl
from jax.experimental.pallas import tpu as pltpu
from jax.sharding import PartitionSpec as P

HW = 10
KW = 21
NB = 27
GW = 8
PIX = 256
ROWS = 64
HALF = 128
SLAB = 32
PITCH = PIX + 8
F32 = jnp.float32
BF16 = jnp.bfloat16


def toeplitz_rows(taps, rows):
    return pltpu.roll(jnp.broadcast_to(taps, (rows, taps.shape[1])), 0, 1, stride=1, stride_axis=0)


def fit_kernel(
    place_ref, own_any, far_any, far_core_any, edge_any, edge_core_any, planes_ref, row_taps_ref, col_taps_ref, mine_ref, theirs_ref,
    own_ref, far_ref, edge_ref, window, col_band, row_band, first, slab_wide, slab, plane, counts, sky_sem,
):
    arriving = [
        pltpu.make_async_copy(source, target, sky_sem.at[k])
        for k, (source, target) in enumerate((
            (own_any, own_ref), (far_any, far_ref.at[0]), (far_core_any, far_ref.at[1]),
            (edge_any, edge_ref.at[0]), (edge_core_any, edge_ref.at[1]),
        ))
    ]
    for copy in arriving:
        copy.start()

    def build(b, carry):
        col = toeplitz_rows(col_taps_ref[pl.ds(b, 1), :], 256)
        col_band[b // 2, :, pl.ds(pl.multiple_of((b % 2) * 128, 128), 128)] = col[:, :128].astype(BF16)
        row_band[b] = toeplitz_rows(row_taps_ref[pl.ds(b, 1), :], 128).astype(BF16)
        return carry

    lax.fori_loop(0, NB + 1, build, 0, unroll=14)

    for copy in arriving:
        copy.wait()
    on_left, on_top = place_ref[0] % 2 == 0, place_ref[0] < 2
    own = own_ref[...].astype(F32)
    quarters = [far_ref[k].astype(F32) for k in range(2)]
    edges = [edge_ref[k].astype(F32) for k in range(2)]
    far = jnp.concatenate([jnp.where(on_left, *quarters), jnp.where(on_left, *quarters[::-1])], 0)
    north, south = jnp.where(on_left, *edges), jnp.where(on_left, *edges[::-1])
    window[...] = jnp.concatenate(
        [north[16 - HW:], jnp.where(on_top, own, far), jnp.where(on_top, far, own), south[:HW],
         jnp.zeros((12, 384), F32)], 0
    ).astype(BF16)

    def columns(pair, carry):
        for half in range(2):
            out = jnp.dot(
                window[:, half * 128:half * 128 + 256], col_band[pair], preferred_element_type=F32
            ).astype(BF16)
            first[2 * pair, :, half * 128:half * 128 + 128] = out[:, :128]
            first[2 * pair + 1, :, half * 128:half * 128 + 128] = out[:, 128:]
        return carry

    lax.fori_loop(0, (NB + 1) // 2, columns, 0, unroll=14)

    for k in range(4):
        for half in range(2):
            slab_wide[half, pl.ds((NB + k) * PITCH, PIX), :] = planes_ref[
                k, :, half * 128:half * 128 + 128
            ].astype(F32)
    for half in range(2):
        slab_wide[half, pl.ds((SLAB - 1) * PITCH, PIX), :] = jnp.zeros((PIX, 128), F32)

    def rows_pass(b, carry):
        for block in range(2):
            out = jnp.dot(
                row_band[b, :, :160], first[b, block * 128:block * 128 + 160, :],
                preferred_element_type=F32,
            )
            for half in range(2):
                slab_wide[half, pl.ds(pl.multiple_of(b * PITCH + block * 128, 8), 128), :] = out[
                    :, half * 128:half * 128 + 128
                ]
        return carry

    lax.fori_loop(0, NB, rows_pass, 0, unroll=27)

    def gram(group, totals):
        totals = list(totals)
        base = pl.multiple_of(group * 8 * SLAB, 8 * SLAB)
        at = pl.multiple_of(group * 8, 8)
        valid = [planes_ref[4 + k, pl.ds(at, 8), :].astype(F32) for k in range(4)]
        for i in range(8):
            here = pl.ds(base + i * SLAB, SLAB)
            there = pl.ds(group * 8 + i, SLAB, stride=PITCH)
            rows = jnp.concatenate([slab_wide[0, there, :], slab_wide[1, there, :]], 1)
            low = rows.astype(BF16)
            slab[here, :] = low
            masked = jnp.concatenate(
                [low * jnp.broadcast_to(v[i:i + 1].astype(BF16), low.shape) for v in valid], 0
            )
            totals[i % 2] = totals[i % 2] + lax.dot_general(
                masked, low, (((1,), (1,)), ((), ())), preferred_element_type=F32
            )
        return tuple(totals)

    matrix = sum(lax.fori_loop(0, PIX // 8, gram, (jnp.zeros((4 * SLAB, SLAB), F32),) * 2, unroll=8)).T

    lane = lax.broadcasted_iota(jnp.int32, (SLAB, 4 * SLAB), 1)
    row = lax.broadcasted_iota(jnp.int32, (SLAB, 4 * SLAB), 0)
    of_exposure = lane // SLAB
    of_basis = lane % SLAB
    def column_of(k):
        return jnp.take_along_axis(matrix, of_exposure * SLAB + k, axis=1)

    for k in range(0, NB - 1, 2):
        here, there = column_of(k), column_of(k + 1)
        inverse = 1.0 / here[k:k + 1]
        ratio = here[k + 1:k + 2] * inverse
        rest = there[k + 1:k + 2] - ratio * there[k:k + 1]
        scaled_there = (matrix[k + 1:k + 2] - ratio * matrix[k:k + 1]) / rest
        scaled_here = (matrix[k:k + 1] - there[k:k + 1] * scaled_there) * inverse
        outside = of_basis[:1] // 2 != k // 2
        matrix = matrix - (
            here * jnp.where(outside, scaled_here, 0.0) + there * jnp.where(outside, scaled_there, 0.0)
        )
    here = column_of(NB - 1)
    matrix = matrix - here * jnp.where(of_basis[:1] == NB - 1, 0.0, matrix[NB - 1:NB] / here[NB - 1:NB])

    def picked(rows):
        return jnp.sum(jnp.where(row == rows, matrix, 0.0), axis=0, keepdims=True)

    right, own, mate = picked(NB + of_exposure), picked(of_basis), picked(of_basis ^ 1)
    beside = lane[:8] ^ 1
    right_b, own_b, mate_b = [
        jnp.take_along_axis(jnp.broadcast_to(v, (8, 4 * SLAB)), beside, axis=1)[:1] for v in (right, own, mate)
    ]
    alone = of_basis[:1] == NB - 1
    mate, mate_b = jnp.where(alone, 0.0, mate), jnp.where(alone, 0.0, mate_b)
    right_b, own_b = jnp.where(alone, 0.0, right_b), jnp.where(alone, 1.0, own_b)
    ratio = mate_b / own
    other = (right_b - ratio * right) / (own_b - ratio * mate)
    solved = (right - mate * other) / own
    solved = jnp.broadcast_to(solved, (8, 4 * SLAB))
    lane8 = lax.broadcasted_iota(jnp.int32, (8, 4 * SLAB), 1)
    row8 = lax.broadcasted_iota(jnp.int32, (8, 4 * SLAB), 0)
    weights = []
    for k in range(4):
        own = -jnp.take_along_axis(solved, lane8 % SLAB + k * SLAB, axis=1)
        own = jnp.where(lane8 % SLAB == NB + k, 1.0, jnp.where(lane8 % SLAB >= NB, 0.0, own))
        weights.append(
            jnp.concatenate([jnp.where(row8 == lane8 // SLAB + 4 * half, own, 0.0) for half in range(2)], 1)
        )
    weights = jnp.concatenate(weights, 0).astype(BF16)

    plane[...] = jnp.zeros_like(plane)

    def residual(group, carry):
        base = pl.multiple_of(group * 8 * SLAB, 8 * SLAB)
        at = pl.multiple_of(group * 8, 8)
        left = jnp.dot(weights, slab[pl.ds(base, 8 * SLAB), :], preferred_element_type=F32)
        total = jnp.zeros((8, PIX), F32)
        seen = jnp.zeros((8, PIX), F32)
        for k in range(4):
            valid = planes_ref[4 + k, pl.ds(at, 8), :].astype(F32)
            seen = seen + valid
            total = total + (valid * left[8 * k:8 * k + 8]).astype(BF16).astype(F32)
        plane[pl.ds(pl.multiple_of(group * 8 + 16, 8), 8), :] = total
        counts[pl.ds(at, 8), :] = seen
        return carry

    lax.fori_loop(0, PIX // 8, residual, 0, unroll=8)

    def block(k):
        side = pl.ds(HALF * (k % 2), HALF)
        return jnp.concatenate(
            [
                plane[16 + 118 * (k // 2):16 + 118 * (k // 2) + HALF + 16, side],
                jnp.concatenate(
                    [counts[ROWS * k:ROWS * k + ROWS, :HALF], counts[ROWS * k:ROWS * k + ROWS, HALF:],
                     jnp.zeros((16, HALF), F32)], 0
                ),
            ],
            1,
        ).astype(BF16)

    for k in range(4):

        @pl.when(place_ref[0] == k)
        def _():
            mine_ref[0], mine_ref[1] = block(k), block(k ^ 2)
            theirs_ref[0], theirs_ref[1] = block(k ^ 1), block(k ^ 3)


def fit(place, skies, planes, row_taps, col_taps):
    vmem = pl.BlockSpec(memory_space=pltpu.VMEM)
    return pl.pallas_call(
        fit_kernel,
        out_shape=[jax.ShapeDtypeStruct((2, HALF + 16, PIX), BF16)] * 2,
        in_specs=[pl.BlockSpec(memory_space=pltpu.SMEM), *[pl.BlockSpec(memory_space=pl.ANY)] * 5] + [vmem] * 3,
        out_specs=[vmem] * 2,
        scratch_shapes=[
            pltpu.VMEM((HALF, 384), BF16),
            pltpu.VMEM((2, ROWS, 384), BF16),
            pltpu.VMEM((2, 16, 384), BF16),
            pltpu.VMEM((288, 384), BF16),
            pltpu.VMEM((14, 256, 256), BF16),
            pltpu.VMEM((28, 128, 256), BF16),
            pltpu.VMEM((28, 288, 256), BF16),
            pltpu.VMEM((2, PITCH * (SLAB + 1), 128), F32),
            pltpu.VMEM((PIX * SLAB, 256), BF16),
            pltpu.VMEM((320, PIX), F32),
            pltpu.VMEM((PIX, PIX), F32),
            pltpu.SemaphoreType.DMA((5,)),
        ],
        compiler_params=pltpu.CompilerParams(vmem_limit_bytes=48 * 1024 * 1024),
        name="fit",
    )(place, *skies, planes, row_taps, col_taps)


def filter_kernel(
    place_ref, near_ref, far_ref, beside_ref, edge_ref, edge_too_ref, row_taps_ref, col_taps_ref,
    keep_ref, give_ref, seen_ref,
):
    on_left, on_top = place_ref[0] % 2 == 0, place_ref[0] < 2
    far = far_ref[...].astype(F32)
    total = near_ref[...] + far[:, :PIX]
    seen = jnp.maximum(total[:HALF, HALF:], 1.0)
    seen_ref[...] = jnp.concatenate([seen[:ROWS], seen[ROWS:]], 1)
    main = total[:HALF + HW, :HALF]
    beside = beside_ref[0] + far[:HALF + HW, PIX:PIX + HW]
    edge = edge_ref[...] + edge_too_ref[...]
    edge = jnp.where(on_left, jnp.concatenate([edge[:, HALF:], edge[:, :HALF]], 1), edge)
    core = jnp.where(on_left, jnp.concatenate([beside, main], 1), jnp.concatenate([main, beside], 1))
    sky = jnp.where(on_top, jnp.concatenate([edge, core], 0), jnp.concatenate([core, edge], 0))
    sky = jnp.concatenate([sky, jnp.zeros((4, HALF + HW), F32)], 0)
    sky = jnp.concatenate([sky, jnp.zeros((HALF + 24, 6), F32)], 1)
    taps = jnp.where(on_left, col_taps_ref[...], pltpu.roll(col_taps_ref[...], HALF + HW, 1))
    col_band = toeplitz_rows(taps, HALF + 16)
    row_band = toeplitz_rows(row_taps_ref[...], HALF)[:, :HALF + 24]
    column_pass = jnp.dot(sky, col_band, precision=lax.Precision.HIGHEST, preferred_element_type=F32)
    lane = lax.broadcasted_iota(jnp.int32, column_pass.shape, 1)
    reached = jnp.logical_and(lane >= jnp.where(on_left, 0, HALF - HW), lane < jnp.where(on_left, HALF + HW, PIX))
    column_pass = jnp.where(reached, column_pass, 0.0)
    part = jnp.dot(row_band, column_pass, precision=lax.Precision.HIGHEST, preferred_element_type=F32)
    keep_ref[...] = jnp.where(on_left, part[:ROWS], part[ROWS:])
    give_ref[...] = jnp.where(on_left, part[ROWS:], part[:ROWS])


def filter_half(place, *operands):
    vmem = pl.BlockSpec(memory_space=pltpu.VMEM)
    return pl.pallas_call(
        filter_kernel,
        out_shape=[jax.ShapeDtypeStruct((ROWS, PIX), F32)] * 3,
        in_specs=[pl.BlockSpec(memory_space=pltpu.SMEM)] + [vmem] * len(operands),
        out_specs=[vmem] * 3,
        compiler_params=pltpu.CompilerParams(vmem_limit_bytes=32 * 1024 * 1024),
        name="filter",
    )(place, *operands)


def routes(tiles, exps):
    core, chip, beside, border, border_too, edge = [], [], [], [], [], []
    for t in range(tiles):
        row, col = t // GW, t % GW
        for e in range(exps):
            here = t * exps + e
            core.append((here, t * exps + (e ^ 1)))
            chip.append((here, t * exps + (e ^ 2)))
            col_to = col + (1 if e % 2 else -1)
            row_to = row + (1 if e // 2 else -1)
            in_cols, in_rows = 0 <= col_to < GW, 0 <= row_to < tiles // GW
            if in_cols:
                beside.append((here, (row * GW + col_to) * exps + (e ^ 1)))
            if in_rows:
                border.append((here, (row_to * GW + col) * exps + (e ^ 2)))
                border_too.append((t * exps + (e ^ 2), (row_to * GW + col) * exps + (e ^ 2)))
                edge.append((here, (row_to * GW + col) * exps + 2 * (e % 2) + 1 - e // 2))
    return core, chip, beside, border, border_too, edge


def send(values, route):
    return lax.ppermute(values, ("tile", "exp"), route)


def rising(taps):
    return jnp.pad(taps, ((0, (-taps.shape[0]) % 4), (0, 256 - KW)))


def falling(taps):
    return jnp.roll(jnp.pad(taps[:, ::-1], ((0, (-taps.shape[0]) % 4), (0, 256 - KW))), 1 - KW, 1)


def shards(template, exposures, masks, basis_rows, basis_cols, psf_row, psf_col):
    core, chip, beside, border, border_too, edge = routes(lax.axis_size("tile"), lax.axis_size("exp"))
    place = lax.axis_index("exp")
    on_left, on_top = place % 2 == 0, place < 2

    own = template[0]
    other = send(own, core)
    strip = jnp.concatenate(
        [jnp.where(on_left, own[:, :HW], other[:, -HW:]), jnp.where(on_left, other[:, :HW], own[:, -HW:])], 0
    )
    strip = send(strip, beside)
    strip, basis_rows, basis_cols = lax.optimization_barrier((strip, basis_rows, basis_cols))
    half = jnp.where(on_left, jnp.concatenate([own, other], 0), jnp.concatenate([other, own], 0))
    strip_core = send(strip, core)
    west, east = jnp.where(on_left, strip, strip_core), jnp.where(on_left, strip_core, strip)
    wide = lax.optimization_barrier(jnp.pad(jnp.concatenate([west, half, east], 1), ((0, 0), (0, 108))))
    wide, exposures, masks = lax.optimization_barrier((wide, exposures, masks))
    planes = jnp.concatenate([exposures[0], masks[0].astype(BF16)], 0)
    far = send(jnp.where(on_left, wide[:ROWS], wide[ROWS:]), chip)
    rows = send(jnp.where(on_top, wide[:16], wide[-16:]), edge)
    far_core, rows_core = send(far, core), send(rows, core)

    rounded = lambda taps: taps.astype(BF16).astype(F32)
    mine, theirs = fit(
        place[None], (wide, far, far_core, rows, rows_core), planes,
        rising(rounded(basis_rows)), falling(rounded(basis_cols)),
    )
    pair = mine.astype(F32) + send(theirs, core).astype(F32)
    main = pair[:, :HALF + HW, :HALF]
    strip = send(jnp.where(on_left, main[:, :, :HW], main[:, :, -HW:]).astype(BF16), beside).astype(F32)
    far = jnp.concatenate([pair[1], jnp.pad(strip[1], ((0, 6), (0, HALF - HW)))], 1).astype(BF16)
    ends = jnp.concatenate([main, strip], 2)
    far, ends = lax.optimization_barrier((far, ends))
    far = send(far, chip)
    rows = send(jnp.where(on_top, ends[0, :HW], ends[0, -HW:]), border)
    rows_too = send(jnp.where(on_top, ends[1, -HW:], ends[1, :HW]), border_too)
    keep, give, seen = filter_half(
        place[None], pair[0], far, strip, rows, rows_too, rising(psf_row[None])[:1], falling(psf_col[None])[:1]
    )
    return ((keep + send(give, core)) / seen)[None]


def solution(mesh):
    placed = (
        P("tile", "exp", None),
        P("tile", "exp", None, None),
        P("tile", "exp", None, None),
        P(),
        P(),
        P(),
        P(),
    )
    return jax.shard_map(
        shards, mesh=mesh, in_specs=placed, out_specs=P("tile", "exp", None), check_vma=False
    )
```

```python
import jax
import jax.numpy as jnp
from jax import lax
from jax.experimental import pallas as pl
from jax.experimental.pallas import tpu as pltpu
from jax.sharding import PartitionSpec as P

HW = 10
KW = 21
NB = 27
GW = 8
PIX = 256
ROWS = 64
HALF = 128
SLAB = 32
PITCH = PIX + 8
F32 = jnp.float32
BF16 = jnp.bfloat16


def toeplitz_rows(taps, rows):
    return pltpu.roll(jnp.broadcast_to(taps, (rows, taps.shape[1])), 0, 1, stride=1, stride_axis=0)


def fit_kernel(
    place_ref, own_any, far_any, far_core_any, edge_any, edge_core_any, planes_ref, row_basis_ref, col_basis_ref, mine_ref, theirs_ref,
    row_taps_ref, col_taps_ref, own_ref, far_ref, edge_ref, window, col_band, row_band, first, slab_wide, slab, plane, counts, sky_sem,
):
    arriving = [
        pltpu.make_async_copy(source, target, sky_sem.at[k])
        for k, (source, target) in enumerate((
            (own_any, own_ref), (far_any, far_ref.at[0]), (far_core_any, far_ref.at[1]),
            (edge_any, edge_ref.at[0]), (edge_core_any, edge_ref.at[1]),
        ))
    ]
    for copy in arriving:
        copy.start()

    def along_lanes(ref):
        taps = jnp.concatenate([ref[...], jnp.zeros((128 - KW, NB), F32)], 0)
        return jnp.transpose(jnp.concatenate([taps, jnp.zeros((128, 128 - NB), F32)], 1))[:SLAB]

    row_taps = along_lanes(row_basis_ref)
    row_taps_ref[...] = jnp.concatenate([row_taps, jnp.zeros_like(row_taps)], 1)
    col_taps = along_lanes(col_basis_ref)
    tap = lax.broadcasted_iota(jnp.int32, (SLAB, 128), 1)
    back = jnp.take_along_axis(col_taps, jnp.minimum(128 - tap, 127), axis=1)
    col_taps_ref[...] = jnp.concatenate(
        [jnp.where(tap == 0, col_taps, 0.0), jnp.where(tap > 128 - KW, back, 0.0)], 1
    )

    def build(b, carry):
        col = toeplitz_rows(col_taps_ref[pl.ds(b, 1), :], 256)
        col_band[b // 2, :, pl.ds(pl.multiple_of((b % 2) * 128, 128), 128)] = col[:, :128].astype(BF16)
        row_band[b] = toeplitz_rows(row_taps_ref[pl.ds(b, 1), :], 128).astype(BF16)
        return carry

    lax.fori_loop(0, NB + 1, build, 0, unroll=14)

    for copy in arriving:
        copy.wait()
    on_left, on_top = place_ref[0] % 2 == 0, place_ref[0] < 2
    own = own_ref[...].astype(F32)
    quarters = [far_ref[k].astype(F32) for k in range(2)]
    edges = [edge_ref[k].astype(F32) for k in range(2)]
    far = jnp.concatenate([jnp.where(on_left, *quarters), jnp.where(on_left, *quarters[::-1])], 0)
    north, south = jnp.where(on_left, *edges), jnp.where(on_left, *edges[::-1])
    window[...] = jnp.concatenate(
        [north[16 - HW:], jnp.where(on_top, own, far), jnp.where(on_top, far, own), south[:HW],
         jnp.zeros((12, 384), F32)], 0
    ).astype(BF16)

    def columns(pair, carry):
        for half in range(2):
            out = jnp.dot(
                window[:, half * 128:half * 128 + 256], col_band[pair], preferred_element_type=F32
            ).astype(BF16)
            first[2 * pair, :, half * 128:half * 128 + 128] = out[:, :128]
            first[2 * pair + 1, :, half * 128:half * 128 + 128] = out[:, 128:]
        return carry

    lax.fori_loop(0, (NB + 1) // 2, columns, 0, unroll=14)

    for k in range(4):
        for half in range(2):
            slab_wide[half, pl.ds((NB + k) * PITCH, PIX), :] = planes_ref[
                k, :, half * 128:half * 128 + 128
            ].astype(F32)
    for half in range(2):
        slab_wide[half, pl.ds((SLAB - 1) * PITCH, PIX), :] = jnp.zeros((PIX, 128), F32)

    def rows_pass(b, carry):
        for block in range(2):
            out = jnp.dot(
                row_band[b, :, :160], first[b, block * 128:block * 128 + 160, :],
                preferred_element_type=F32,
            )
            for half in range(2):
                slab_wide[half, pl.ds(pl.multiple_of(b * PITCH + block * 128, 8), 128), :] = out[
                    :, half * 128:half * 128 + 128
                ]
        return carry

    lax.fori_loop(0, NB, rows_pass, 0, unroll=27)

    def gram(group, totals):
        totals = list(totals)
        base = pl.multiple_of(group * 8 * SLAB, 8 * SLAB)
        at = pl.multiple_of(group * 8, 8)
        valid = [planes_ref[4 + k, pl.ds(at, 8), :].astype(F32) for k in range(4)]
        for i in range(8):
            here = pl.ds(base + i * SLAB, SLAB)
            there = pl.ds(group * 8 + i, SLAB, stride=PITCH)
            rows = jnp.concatenate([slab_wide[0, there, :], slab_wide[1, there, :]], 1)
            low = rows.astype(BF16)
            slab[here, :] = low
            masked = jnp.concatenate(
                [low * jnp.broadcast_to(v[i:i + 1].astype(BF16), low.shape) for v in valid], 0
            )
            totals[i % 2] = totals[i % 2] + lax.dot_general(
                masked, low, (((1,), (1,)), ((), ())), preferred_element_type=F32
            )
        return tuple(totals)

    matrix = sum(lax.fori_loop(0, PIX // 8, gram, (jnp.zeros((4 * SLAB, SLAB), F32),) * 2, unroll=16)).T

    lane = lax.broadcasted_iota(jnp.int32, (SLAB, 4 * SLAB), 1)
    row = lax.broadcasted_iota(jnp.int32, (SLAB, 4 * SLAB), 0)
    of_exposure = lane // SLAB
    of_basis = lane % SLAB
    def column_of(k):
        return jnp.take_along_axis(matrix, of_exposure * SLAB + k, axis=1)

    for k in range(0, NB - 1, 2):
        here, there = column_of(k), column_of(k + 1)
        inverse = 1.0 / here[k:k + 1]
        ratio = here[k + 1:k + 2] * inverse
        rest = there[k + 1:k + 2] - ratio * there[k:k + 1]
        scaled_there = (matrix[k + 1:k + 2] - ratio * matrix[k:k + 1]) / rest
        scaled_here = (matrix[k:k + 1] - there[k:k + 1] * scaled_there) * inverse
        outside = of_basis[:1] // 2 != k // 2
        matrix = matrix - (
            here * jnp.where(outside, scaled_here, 0.0) + there * jnp.where(outside, scaled_there, 0.0)
        )
    here = column_of(NB - 1)
    matrix = matrix - here * jnp.where(of_basis[:1] == NB - 1, 0.0, matrix[NB - 1:NB] / here[NB - 1:NB])

    def picked(rows):
        return jnp.sum(jnp.where(row == rows, matrix, 0.0), axis=0, keepdims=True)

    right, own, mate = picked(NB + of_exposure), picked(of_basis), picked(of_basis ^ 1)
    beside = lane[:8] ^ 1
    right_b, own_b, mate_b = [
        jnp.take_along_axis(jnp.broadcast_to(v, (8, 4 * SLAB)), beside, axis=1)[:1] for v in (right, own, mate)
    ]
    alone = of_basis[:1] == NB - 1
    mate, mate_b = jnp.where(alone, 0.0, mate), jnp.where(alone, 0.0, mate_b)
    right_b, own_b = jnp.where(alone, 0.0, right_b), jnp.where(alone, 1.0, own_b)
    ratio = mate_b / own
    other = (right_b - ratio * right) / (own_b - ratio * mate)
    solved = (right - mate * other) / own
    solved = jnp.broadcast_to(solved, (8, 4 * SLAB))
    lane8 = lax.broadcasted_iota(jnp.int32, (8, 4 * SLAB), 1)
    row8 = lax.broadcasted_iota(jnp.int32, (8, 4 * SLAB), 0)
    weights = []
    for k in range(4):
        own = -jnp.take_along_axis(solved, lane8 % SLAB + k * SLAB, axis=1)
        own = jnp.where(lane8 % SLAB == NB + k, 1.0, jnp.where(lane8 % SLAB >= NB, 0.0, own))
        weights.append(
            jnp.concatenate([jnp.where(row8 == lane8 // SLAB + 4 * half, own, 0.0) for half in range(2)], 1)
        )
    weights = jnp.concatenate(weights, 0).astype(BF16)

    plane[...] = jnp.zeros_like(plane)

    def residual(group, carry):
        base = pl.multiple_of(group * 8 * SLAB, 8 * SLAB)
        at = pl.multiple_of(group * 8, 8)
        left = jnp.dot(weights, slab[pl.ds(base, 8 * SLAB), :], preferred_element_type=F32)
        total = jnp.zeros((8, PIX), F32)
        seen = jnp.zeros((8, PIX), F32)
        for k in range(4):
            valid = planes_ref[4 + k, pl.ds(at, 8), :].astype(F32)
            seen = seen + valid
            total = total + (valid * left[8 * k:8 * k + 8]).astype(BF16).astype(F32)
        plane[pl.ds(pl.multiple_of(group * 8 + 16, 8), 8), :] = total
        counts[pl.ds(at, 8), :] = seen
        return carry

    lax.fori_loop(0, PIX // 8, residual, 0, unroll=16)

    def block(k):
        side = pl.ds(HALF * (k % 2), HALF)
        return jnp.concatenate(
            [
                plane[16 + 118 * (k // 2):16 + 118 * (k // 2) + HALF + 16, side],
                jnp.concatenate(
                    [counts[ROWS * k:ROWS * k + ROWS, :HALF], counts[ROWS * k:ROWS * k + ROWS, HALF:],
                     jnp.zeros((16, HALF), F32)], 0
                ),
            ],
            1,
        ).astype(BF16)

    for k in range(4):

        @pl.when(place_ref[0] == k)
        def _():
            mine_ref[0], mine_ref[1] = block(k), block(k ^ 2)
            theirs_ref[0], theirs_ref[1] = block(k ^ 1), block(k ^ 3)


def fit(place, skies, planes, row_taps, col_taps):
    vmem = pl.BlockSpec(memory_space=pltpu.VMEM)
    return pl.pallas_call(
        fit_kernel,
        out_shape=[jax.ShapeDtypeStruct((2, HALF + 16, PIX), BF16)] * 2,
        in_specs=[pl.BlockSpec(memory_space=pltpu.SMEM), *[pl.BlockSpec(memory_space=pl.ANY)] * 5] + [vmem] * 3,
        out_specs=[vmem] * 2,
        scratch_shapes=[
            pltpu.VMEM((SLAB, 256), F32),
            pltpu.VMEM((SLAB, 256), F32),
            pltpu.VMEM((HALF, 384), BF16),
            pltpu.VMEM((2, ROWS, 384), BF16),
            pltpu.VMEM((2, 16, 384), BF16),
            pltpu.VMEM((288, 384), BF16),
            pltpu.VMEM((14, 256, 256), BF16),
            pltpu.VMEM((28, 128, 256), BF16),
            pltpu.VMEM((28, 288, 256), BF16),
            pltpu.VMEM((2, PITCH * (SLAB + 1), 128), F32),
            pltpu.VMEM((PIX * SLAB, 256), BF16),
            pltpu.VMEM((320, PIX), F32),
            pltpu.VMEM((PIX, PIX), F32),
            pltpu.SemaphoreType.DMA((5,)),
        ],
        compiler_params=pltpu.CompilerParams(vmem_limit_bytes=48 * 1024 * 1024),
        name="fit",
    )(place, *skies, planes, row_taps, col_taps)


def filter_kernel(
    place_ref, near_ref, far_ref, beside_ref, edge_ref, edge_too_ref, row_taps_ref, col_taps_ref,
    keep_ref, give_ref, seen_ref,
):
    on_left, on_top = place_ref[0] % 2 == 0, place_ref[0] < 2
    far = far_ref[...].astype(F32)
    total = near_ref[...] + far[:, :PIX]
    seen = jnp.maximum(total[:HALF, HALF:], 1.0)
    seen_ref[...] = jnp.concatenate([seen[:ROWS], seen[ROWS:]], 1)
    main = total[:HALF + HW, :HALF]
    beside = beside_ref[0] + far[:HALF + HW, PIX:PIX + HW]
    edge = edge_ref[...] + edge_too_ref[...]
    edge = jnp.where(on_left, jnp.concatenate([edge[:, HALF:], edge[:, :HALF]], 1), edge)
    core = jnp.where(on_left, jnp.concatenate([beside, main], 1), jnp.concatenate([main, beside], 1))
    sky = jnp.where(on_top, jnp.concatenate([edge, core], 0), jnp.concatenate([core, edge], 0))
    sky = jnp.concatenate([sky, jnp.zeros((4, HALF + HW), F32)], 0)
    sky = jnp.concatenate([sky, jnp.zeros((HALF + 24, 6), F32)], 1)
    taps = jnp.where(on_left, col_taps_ref[...], pltpu.roll(col_taps_ref[...], HALF + HW, 1))
    col_band = toeplitz_rows(taps, HALF + 16)
    row_band = toeplitz_rows(row_taps_ref[...], HALF)[:, :HALF + 24]
    column_pass = jnp.dot(sky, col_band, precision=lax.Precision.HIGHEST, preferred_element_type=F32)
    lane = lax.broadcasted_iota(jnp.int32, column_pass.shape, 1)
    reached = jnp.logical_and(lane >= jnp.where(on_left, 0, HALF - HW), lane < jnp.where(on_left, HALF + HW, PIX))
    column_pass = jnp.where(reached, column_pass, 0.0)
    part = jnp.dot(row_band, column_pass, precision=lax.Precision.HIGHEST, preferred_element_type=F32)
    keep_ref[...] = jnp.where(on_left, part[:ROWS], part[ROWS:])
    give_ref[...] = jnp.where(on_left, part[ROWS:], part[:ROWS])


def filter_half(place, *operands):
    vmem = pl.BlockSpec(memory_space=pltpu.VMEM)
    return pl.pallas_call(
        filter_kernel,
        out_shape=[jax.ShapeDtypeStruct((ROWS, PIX), F32)] * 3,
        in_specs=[pl.BlockSpec(memory_space=pltpu.SMEM)] + [vmem] * len(operands),
        out_specs=[vmem] * 3,
        compiler_params=pltpu.CompilerParams(vmem_limit_bytes=32 * 1024 * 1024),
        name="filter",
    )(place, *operands)


def routes(tiles, exps):
    core, chip, beside, border, border_too, edge = [], [], [], [], [], []
    for t in range(tiles):
        row, col = t // GW, t % GW
        for e in range(exps):
            here = t * exps + e
            core.append((here, t * exps + (e ^ 1)))
            chip.append((here, t * exps + (e ^ 2)))
            col_to = col + (1 if e % 2 else -1)
            row_to = row + (1 if e // 2 else -1)
            in_cols, in_rows = 0 <= col_to < GW, 0 <= row_to < tiles // GW
            if in_cols:
                beside.append((here, (row * GW + col_to) * exps + (e ^ 1)))
            if in_rows:
                border.append((here, (row_to * GW + col) * exps + (e ^ 2)))
                border_too.append((t * exps + (e ^ 2), (row_to * GW + col) * exps + (e ^ 2)))
                edge.append((here, (row_to * GW + col) * exps + 2 * (e % 2) + 1 - e // 2))
    return core, chip, beside, border, border_too, edge


def send(values, route):
    return lax.ppermute(values, ("tile", "exp"), route)


def rising(taps):
    return jnp.pad(taps, ((0, (-taps.shape[0]) % 4), (0, 256 - KW)))


def falling(taps):
    return jnp.roll(jnp.pad(taps[:, ::-1], ((0, (-taps.shape[0]) % 4), (0, 256 - KW))), 1 - KW, 1)


def shards(template, exposures, masks, basis_rows, basis_cols, psf_row, psf_col):
    core, chip, beside, border, border_too, edge = routes(lax.axis_size("tile"), lax.axis_size("exp"))
    place = lax.axis_index("exp")
    on_left, on_top = place % 2 == 0, place < 2

    own = template[0]
    other = send(own, core)
    strip = jnp.concatenate(
        [jnp.where(on_left, own[:, :HW], other[:, -HW:]), jnp.where(on_left, other[:, :HW], own[:, -HW:])], 0
    )
    strip = send(strip, beside)
    half = jnp.where(on_left, jnp.concatenate([own, other], 0), jnp.concatenate([other, own], 0))
    strip_core = send(strip, core)
    west, east = jnp.where(on_left, strip, strip_core), jnp.where(on_left, strip_core, strip)
    wide = lax.optimization_barrier(jnp.pad(jnp.concatenate([west, half, east], 1), ((0, 0), (0, 108))))
    wide, exposures, masks = lax.optimization_barrier((wide, exposures, masks))
    planes = jnp.concatenate([exposures[0], masks[0].astype(BF16)], 0)
    far = send(jnp.where(on_left, wide[:ROWS], wide[ROWS:]), chip)
    rows = send(jnp.where(on_top, wide[:16], wide[-16:]), edge)
    far_core, rows_core = send(far, core), send(rows, core)

    mine, theirs = fit(
        place[None], (wide, far, far_core, rows, rows_core), planes,
        basis_rows.T, basis_cols.T,
    )
    pair = mine.astype(F32) + send(theirs, core).astype(F32)
    main = pair[:, :HALF + HW, :HALF]
    strip = send(jnp.where(on_left, main[:, :, :HW], main[:, :, -HW:]).astype(BF16), beside).astype(F32)
    far = jnp.concatenate([pair[1], jnp.pad(strip[1], ((0, 6), (0, HALF - HW)))], 1).astype(BF16)
    ends = jnp.concatenate([main, strip], 2)
    far, ends = lax.optimization_barrier((far, ends))
    far = send(far, chip)
    rows = send(jnp.where(on_top, ends[0, :HW], ends[0, -HW:]), border)
    rows_too = send(jnp.where(on_top, ends[1, -HW:], ends[1, :HW]), border_too)
    keep, give, seen = filter_half(
        place[None], pair[0], far, strip, rows, rows_too, rising(psf_row[None])[:1], falling(psf_col[None])[:1]
    )
    return ((keep + send(give, core)) / seen)[None]


def solution(mesh):
    placed = (
        P("tile", "exp", None),
        P("tile", "exp", None, None),
        P("tile", "exp", None, None),
        P(),
        P(),
        P(),
        P(),
    )
    return jax.shard_map(
        shards, mesh=mesh, in_specs=placed, out_specs=P("tile", "exp", None), check_vma=False
    )
```

```python
import jax
import jax.numpy as jnp
from jax import lax
from jax.experimental import pallas as pl
from jax.experimental.pallas import tpu as pltpu
from jax.sharding import PartitionSpec as P

HW = 10
KW = 21
NB = 27
GW = 8
PIX = 256
ROWS = 64
HALF = 128
SLAB = 32
PITCH = PIX + 8
F32 = jnp.float32
BF16 = jnp.bfloat16


def toeplitz_rows(taps, rows):
    return pltpu.roll(jnp.broadcast_to(taps, (rows, taps.shape[1])), 0, 1, stride=1, stride_axis=0)


def fit_kernel(
    place_ref, own_any, far_any, far_core_any, edge_any, edge_core_any, planes_ref, row_basis_ref, col_basis_ref, mine_ref, theirs_ref,
    row_taps_ref, col_taps_ref, own_ref, far_ref, edge_ref, window, col_band, row_band, first, slab_wide, slab, plane, counts, sky_sem,
):
    arriving = [
        pltpu.make_async_copy(source, target, sky_sem.at[k])
        for k, (source, target) in enumerate((
            (own_any, own_ref), (far_any, far_ref.at[0]), (far_core_any, far_ref.at[1]),
            (edge_any, edge_ref.at[0]), (edge_core_any, edge_ref.at[1]),
        ))
    ]
    for copy in arriving:
        copy.start()

    def along_lanes(ref):
        taps = jnp.concatenate([ref[...], jnp.zeros((128 - KW, NB), F32)], 0)
        return jnp.transpose(jnp.concatenate([taps, jnp.zeros((128, 128 - NB), F32)], 1))[:SLAB]

    row_taps = along_lanes(row_basis_ref)
    row_taps_ref[...] = jnp.concatenate([row_taps, jnp.zeros_like(row_taps)], 1)
    col_taps = along_lanes(col_basis_ref)
    tap = lax.broadcasted_iota(jnp.int32, (SLAB, 128), 1)
    back = jnp.take_along_axis(col_taps, jnp.minimum(128 - tap, 127), axis=1)
    col_taps_ref[...] = jnp.concatenate(
        [jnp.where(tap == 0, col_taps, 0.0), jnp.where(tap > 128 - KW, back, 0.0)], 1
    )

    def build(b, carry):
        col = toeplitz_rows(col_taps_ref[pl.ds(b, 1), :], 256)
        col_band[b // 2, :, pl.ds(pl.multiple_of((b % 2) * 128, 128), 128)] = col[:, :128].astype(BF16)
        row_band[b] = toeplitz_rows(row_taps_ref[pl.ds(b, 1), :], 128).astype(BF16)
        return carry

    lax.fori_loop(0, NB + 1, build, 0, unroll=14)

    for copy in arriving:
        copy.wait()
    on_left, on_top = place_ref[0] % 2 == 0, place_ref[0] < 2
    own = own_ref[...].astype(F32)
    quarters = [far_ref[k].astype(F32) for k in range(2)]
    edges = [edge_ref[k].astype(F32) for k in range(2)]
    far = jnp.concatenate([jnp.where(on_left, *quarters), jnp.where(on_left, *quarters[::-1])], 0)
    north, south = jnp.where(on_left, *edges), jnp.where(on_left, *edges[::-1])
    window[...] = jnp.concatenate(
        [north[16 - HW:], jnp.where(on_top, own, far), jnp.where(on_top, far, own), south[:HW],
         jnp.zeros((12, 384), F32)], 0
    ).astype(BF16)

    def columns(pair, carry):
        for half in range(2):
            out = jnp.dot(
                window[:, half * 128:half * 128 + 256], col_band[pair], preferred_element_type=F32
            ).astype(BF16)
            first[2 * pair, :, half * 128:half * 128 + 128] = out[:, :128]
            first[2 * pair + 1, :, half * 128:half * 128 + 128] = out[:, 128:]
        return carry

    lax.fori_loop(0, (NB + 1) // 2, columns, 0, unroll=14)

    for k in range(4):
        for half in range(2):
            slab_wide[half, pl.ds((NB + k) * PITCH, PIX), :] = planes_ref[
                k, :, half * 128:half * 128 + 128
            ].astype(F32)
    for half in range(2):
        slab_wide[half, pl.ds((SLAB - 1) * PITCH, PIX), :] = jnp.zeros((PIX, 128), F32)

    def rows_pass(b, carry):
        for block in range(2):
            out = jnp.dot(
                row_band[b, :, :160], first[b, block * 128:block * 128 + 160, :],
                preferred_element_type=F32,
            )
            for half in range(2):
                slab_wide[half, pl.ds(pl.multiple_of(b * PITCH + block * 128, 8), 128), :] = out[
                    :, half * 128:half * 128 + 128
                ]
        return carry

    lax.fori_loop(0, NB, rows_pass, 0, unroll=27)

    def gram(group, totals):
        totals = list(totals)
        base = pl.multiple_of(group * 8 * SLAB, 8 * SLAB)
        at = pl.multiple_of(group * 8, 8)
        valid = [planes_ref[4 + k, pl.ds(at, 8), :].astype(F32) for k in range(4)]
        for i in range(8):
            here = pl.ds(base + i * SLAB, SLAB)
            there = pl.ds(group * 8 + i, SLAB, stride=PITCH)
            rows = jnp.concatenate([slab_wide[0, there, :], slab_wide[1, there, :]], 1)
            low = rows.astype(BF16)
            slab[here, :] = low
            masked = jnp.concatenate(
                [low * jnp.broadcast_to(v[i:i + 1].astype(BF16), low.shape) for v in valid], 0
            )
            totals[i % 2] = totals[i % 2] + lax.dot_general(
                masked, low, (((1,), (1,)), ((), ())), preferred_element_type=F32
            )
        return tuple(totals)

    matrix = sum(lax.fori_loop(0, PIX // 8, gram, (jnp.zeros((4 * SLAB, SLAB), F32),) * 2, unroll=16)).T

    lane = lax.broadcasted_iota(jnp.int32, (SLAB, 4 * SLAB), 1)
    row = lax.broadcasted_iota(jnp.int32, (SLAB, 4 * SLAB), 0)
    of_exposure = lane // SLAB
    of_basis = lane % SLAB
    def column_of(k):
        return jnp.take_along_axis(matrix, of_exposure * SLAB + k, axis=1)

    for k in range(0, NB - 1, 2):
        here, there = column_of(k), column_of(k + 1)
        inverse = 1.0 / here[k:k + 1]
        ratio = here[k + 1:k + 2] * inverse
        rest = there[k + 1:k + 2] - ratio * there[k:k + 1]
        scaled_there = (matrix[k + 1:k + 2] - ratio * matrix[k:k + 1]) / rest
        scaled_here = (matrix[k:k + 1] - there[k:k + 1] * scaled_there) * inverse
        outside = of_basis[:1] // 2 != k // 2
        matrix = matrix - (
            here * jnp.where(outside, scaled_here, 0.0) + there * jnp.where(outside, scaled_there, 0.0)
        )
    here = column_of(NB - 1)
    matrix = matrix - here * jnp.where(of_basis[:1] == NB - 1, 0.0, matrix[NB - 1:NB] / here[NB - 1:NB])

    def picked(rows):
        return jnp.sum(jnp.where(row == rows, matrix, 0.0), axis=0, keepdims=True)

    right, own, mate = picked(NB + of_exposure), picked(of_basis), picked(of_basis ^ 1)
    beside = lane[:8] ^ 1
    right_b, own_b, mate_b = [
        jnp.take_along_axis(jnp.broadcast_to(v, (8, 4 * SLAB)), beside, axis=1)[:1] for v in (right, own, mate)
    ]
    alone = of_basis[:1] == NB - 1
    mate, mate_b = jnp.where(alone, 0.0, mate), jnp.where(alone, 0.0, mate_b)
    right_b, own_b = jnp.where(alone, 0.0, right_b), jnp.where(alone, 1.0, own_b)
    ratio = mate_b / own
    other = (right_b - ratio * right) / (own_b - ratio * mate)
    solved = (right - mate * other) / own
    solved = jnp.broadcast_to(solved, (8, 4 * SLAB))
    lane8 = lax.broadcasted_iota(jnp.int32, (8, 4 * SLAB), 1)
    row8 = lax.broadcasted_iota(jnp.int32, (8, 4 * SLAB), 0)
    weights = []
    for k in range(4):
        own = -jnp.take_along_axis(solved, lane8 % SLAB + k * SLAB, axis=1)
        own = jnp.where(lane8 % SLAB == NB + k, 1.0, jnp.where(lane8 % SLAB >= NB, 0.0, own))
        weights.append(
            jnp.concatenate([jnp.where(row8 == lane8 // SLAB + 4 * half, own, 0.0) for half in range(2)], 1)
        )
    weights = jnp.concatenate(weights, 0).astype(BF16)

    plane[...] = jnp.zeros_like(plane)

    def residual(group, carry):
        base = pl.multiple_of(group * 8 * SLAB, 8 * SLAB)
        at = pl.multiple_of(group * 8, 8)
        left = jnp.dot(weights, slab[pl.ds(base, 8 * SLAB), :], preferred_element_type=F32)
        total = jnp.zeros((8, PIX), F32)
        seen = jnp.zeros((8, PIX), F32)
        for k in range(4):
            valid = planes_ref[4 + k, pl.ds(at, 8), :].astype(F32)
            seen = seen + valid
            total = total + (valid * left[8 * k:8 * k + 8]).astype(BF16).astype(F32)
        plane[pl.ds(pl.multiple_of(group * 8 + 16, 8), 8), :] = total
        counts[pl.ds(at, 8), :] = seen
        return carry

    lax.fori_loop(0, PIX // 8, residual, 0, unroll=32)

    def block(k):
        side = pl.ds(HALF * (k % 2), HALF)
        return jnp.concatenate(
            [
                plane[16 + 118 * (k // 2):16 + 118 * (k // 2) + HALF + 16, side],
                jnp.concatenate(
                    [counts[ROWS * k:ROWS * k + ROWS, :HALF], counts[ROWS * k:ROWS * k + ROWS, HALF:],
                     jnp.zeros((16, HALF), F32)], 0
                ),
            ],
            1,
        ).astype(BF16)

    for k in range(4):

        @pl.when(place_ref[0] == k)
        def _():
            mine_ref[0], mine_ref[1] = block(k), block(k ^ 2)
            theirs_ref[0], theirs_ref[1] = block(k ^ 1), block(k ^ 3)


def fit(place, skies, planes, row_taps, col_taps):
    vmem = pl.BlockSpec(memory_space=pltpu.VMEM)
    return pl.pallas_call(
        fit_kernel,
        out_shape=[jax.ShapeDtypeStruct((2, HALF + 16, PIX), BF16)] * 2,
        in_specs=[pl.BlockSpec(memory_space=pltpu.SMEM), *[pl.BlockSpec(memory_space=pl.ANY)] * 5] + [vmem] * 3,
        out_specs=[vmem] * 2,
        scratch_shapes=[
            pltpu.VMEM((SLAB, 256), F32),
            pltpu.VMEM((SLAB, 256), F32),
            pltpu.VMEM((HALF, 384), BF16),
            pltpu.VMEM((2, ROWS, 384), BF16),
            pltpu.VMEM((2, 16, 384), BF16),
            pltpu.VMEM((288, 384), BF16),
            pltpu.VMEM((14, 256, 256), BF16),
            pltpu.VMEM((28, 128, 256), BF16),
            pltpu.VMEM((28, 288, 256), BF16),
            pltpu.VMEM((2, PITCH * (SLAB + 1), 128), F32),
            pltpu.VMEM((PIX * SLAB, 256), BF16),
            pltpu.VMEM((320, PIX), F32),
            pltpu.VMEM((PIX, PIX), F32),
            pltpu.SemaphoreType.DMA((5,)),
        ],
        compiler_params=pltpu.CompilerParams(vmem_limit_bytes=48 * 1024 * 1024),
        name="fit",
    )(place, *skies, planes, row_taps, col_taps)


def filter_kernel(
    place_ref, near_ref, far_ref, beside_ref, edge_ref, edge_too_ref, row_taps_ref, col_taps_ref,
    keep_ref, give_ref, seen_ref,
):
    on_left, on_top = place_ref[0] % 2 == 0, place_ref[0] < 2
    far = far_ref[...].astype(F32)
    total = near_ref[...] + far[:, :PIX]
    seen = jnp.maximum(total[:HALF, HALF:], 1.0)
    seen_ref[...] = jnp.concatenate([seen[:ROWS], seen[ROWS:]], 1)
    main = total[:HALF + HW, :HALF]
    beside = beside_ref[0] + far[:HALF + HW, PIX:PIX + HW]
    edge = edge_ref[...] + edge_too_ref[...]
    edge = jnp.where(on_left, jnp.concatenate([edge[:, HALF:], edge[:, :HALF]], 1), edge)
    core = jnp.where(on_left, jnp.concatenate([beside, main], 1), jnp.concatenate([main, beside], 1))
    sky = jnp.where(on_top, jnp.concatenate([edge, core], 0), jnp.concatenate([core, edge], 0))
    sky = jnp.concatenate([sky, jnp.zeros((4, HALF + HW), F32)], 0)
    sky = jnp.concatenate([sky, jnp.zeros((HALF + 24, 6), F32)], 1)
    taps = jnp.where(on_left, col_taps_ref[...], pltpu.roll(col_taps_ref[...], HALF + HW, 1))
    col_band = toeplitz_rows(taps, HALF + 16)
    row_band = toeplitz_rows(row_taps_ref[...], HALF)[:, :HALF + 24]
    column_pass = jnp.dot(sky, col_band, precision=lax.Precision.HIGHEST, preferred_element_type=F32)
    lane = lax.broadcasted_iota(jnp.int32, column_pass.shape, 1)
    reached = jnp.logical_and(lane >= jnp.where(on_left, 0, HALF - HW), lane < jnp.where(on_left, HALF + HW, PIX))
    column_pass = jnp.where(reached, column_pass, 0.0)
    part = jnp.dot(row_band, column_pass, precision=lax.Precision.HIGHEST, preferred_element_type=F32)
    keep_ref[...] = jnp.where(on_left, part[:ROWS], part[ROWS:])
    give_ref[...] = jnp.where(on_left, part[ROWS:], part[:ROWS])


def filter_half(place, *operands):
    vmem = pl.BlockSpec(memory_space=pltpu.VMEM)
    return pl.pallas_call(
        filter_kernel,
        out_shape=[jax.ShapeDtypeStruct((ROWS, PIX), F32)] * 3,
        in_specs=[pl.BlockSpec(memory_space=pltpu.SMEM)] + [vmem] * len(operands),
        out_specs=[vmem] * 3,
        compiler_params=pltpu.CompilerParams(vmem_limit_bytes=32 * 1024 * 1024),
        name="filter",
    )(place, *operands)


def routes(tiles, exps):
    core, chip, beside, border, border_too, edge = [], [], [], [], [], []
    for t in range(tiles):
        row, col = t // GW, t % GW
        for e in range(exps):
            here = t * exps + e
            core.append((here, t * exps + (e ^ 1)))
            chip.append((here, t * exps + (e ^ 2)))
            col_to = col + (1 if e % 2 else -1)
            row_to = row + (1 if e // 2 else -1)
            in_cols, in_rows = 0 <= col_to < GW, 0 <= row_to < tiles // GW
            if in_cols:
                beside.append((here, (row * GW + col_to) * exps + (e ^ 1)))
            if in_rows:
                border.append((here, (row_to * GW + col) * exps + (e ^ 2)))
                border_too.append((t * exps + (e ^ 2), (row_to * GW + col) * exps + (e ^ 2)))
                edge.append((here, (row_to * GW + col) * exps + 2 * (e % 2) + 1 - e // 2))
    return core, chip, beside, border, border_too, edge


def send(values, route):
    return lax.ppermute(values, ("tile", "exp"), route)


def rising(taps):
    return jnp.pad(taps, ((0, (-taps.shape[0]) % 4), (0, 256 - KW)))


def falling(taps):
    return jnp.roll(jnp.pad(taps[:, ::-1], ((0, (-taps.shape[0]) % 4), (0, 256 - KW))), 1 - KW, 1)


def shards(template, exposures, masks, basis_rows, basis_cols, psf_row, psf_col):
    core, chip, beside, border, border_too, edge = routes(lax.axis_size("tile"), lax.axis_size("exp"))
    place = lax.axis_index("exp")
    on_left, on_top = place % 2 == 0, place < 2

    own = template[0]
    other = send(own, core)
    strip = jnp.concatenate(
        [jnp.where(on_left, own[:, :HW], other[:, -HW:]), jnp.where(on_left, other[:, :HW], own[:, -HW:])], 0
    )
    strip = send(strip, beside)
    half = jnp.where(on_left, jnp.concatenate([own, other], 0), jnp.concatenate([other, own], 0))
    strip_core = send(strip, core)
    west, east = jnp.where(on_left, strip, strip_core), jnp.where(on_left, strip_core, strip)
    wide = lax.optimization_barrier(jnp.pad(jnp.concatenate([west, half, east], 1), ((0, 0), (0, 108))))
    wide, exposures, masks = lax.optimization_barrier((wide, exposures, masks))
    planes = jnp.concatenate([exposures[0], masks[0].astype(BF16)], 0)
    far = send(jnp.where(on_left, wide[:ROWS], wide[ROWS:]), chip)
    rows = send(jnp.where(on_top, wide[:16], wide[-16:]), edge)
    far_core, rows_core = send(far, core), send(rows, core)

    mine, theirs = fit(
        place[None], (wide, far, far_core, rows, rows_core), planes,
        basis_rows.T, basis_cols.T,
    )
    pair = mine.astype(F32) + send(theirs, core).astype(F32)
    main = pair[:, :HALF + HW, :HALF]
    strip = send(jnp.where(on_left, main[:, :, :HW], main[:, :, -HW:]).astype(BF16), beside).astype(F32)
    far = jnp.concatenate([pair[1], jnp.pad(strip[1], ((0, 6), (0, HALF - HW)))], 1).astype(BF16)
    ends = jnp.concatenate([main, strip], 2)
    far, ends = lax.optimization_barrier((far, ends))
    far = send(far, chip)
    rows = send(jnp.where(on_top, ends[0, :HW], ends[0, -HW:]), border)
    rows_too = send(jnp.where(on_top, ends[1, -HW:], ends[1, :HW]), border_too)
    keep, give, seen = filter_half(
        place[None], pair[0], far, strip, rows, rows_too, rising(psf_row[None])[:1], falling(psf_col[None])[:1]
    )
    return ((keep + send(give, core)) / seen)[None]


def solution(mesh):
    placed = (
        P("tile", "exp", None),
        P("tile", "exp", None, None),
        P("tile", "exp", None, None),
        P(),
        P(),
        P(),
        P(),
    )
    return jax.shard_map(
        shards, mesh=mesh, in_specs=placed, out_specs=P("tile", "exp", None), check_vma=False
    )
```
